128 devices in a mesh: gz: 128 (over z, x, y, core).
Axes of the slice: x: 4, y: 4, z: 4, core: 2. Of those that a mesh axis runs over, the one named last changes fastest.
Arguments:
- features: bfloat16 [4096, 64, 512], P('gz'), may hold values from -6 to 6
- counts: int32 [128], P('gz'), may hold values from 2 to 30, as said below
- neighbors: int32 [6, 4096], P(None, 'gz'), may hold values from -1 to 4095, as said below
- weight_one: bfloat16 [27, 64, 64], replicated, may hold values from -0.15625 to 0.15625
- weight_two: bfloat16 [27, 64, 64], replicated, may hold values from -0.15625 to 0.15625
- scale_one: float32 [64], replicated, may hold values from 0.1 to 1.9
- shift_one: float32 [64], replicated, may hold values from -3 to 3
- scale_two: float32 [64], replicated, may hold values from 0.1 to 1.9
- shift_two: float32 [64], replicated, may hold values from -3 to 3
Outputs:
- bricks_out: bfloat16 [4096, 64, 512], P('gz')
The draws below stay inside these ranges and needn't reach their ends.
Inputs may be any that keep to these rules, and one draw needn't show every extreme that they name: `counts`: device i and device i + 64 hold together at most 32 live bricks, and some such pair holds exactly 32. A device's live bricks are its slots below its count. Only live bricks have and are neighbors. Symmetric: if neighbors[k, g] = h then neighbors[k xor 1, h] = g. Two different devices share at most one face. Device i shares a face with devices i + d and i - d modulo 128 for d = 1 to 5, and with device i + 128 / 2 modulo 128, and with no others.
All inputs are finite; a program needn't handle non-finite values.
Results may differ from the reference program's by a relative error of at most 0.0038.
Values may be sent and summed in bfloat16 or wider, within the bound.
A program may use at most 128 MiB of HBM per device.

```python
import jax
import jax.numpy as jnp
from jax import lax

C = 64
BR = 8
CAP = 32
LINKS = 6
NB = 4096
LOWC = 2
N_GZ = 128


def brick_counts(key):
    key = jax.random.fold_in(key, 101)
    key_list = jax.random.split(key, 4)
    pair_count = N_GZ // 2
    lowest = max(2 * LOWC, CAP - CAP // 4)
    totals = jax.random.randint(key_list[0], (pair_count,), lowest, CAP + 1)
    chosen = jax.random.randint(key_list[1], (), 0, pair_count)
    marker = jnp.arange(pair_count) == chosen
    totals = jnp.where(marker, CAP, totals)
    spread = jax.random.randint(key_list[2], (pair_count,), 0, 1 << 20)
    leading = LOWC + spread % (totals - 2 * LOWC + 1)
    leading = jnp.where(marker, CAP - LOWC, leading)
    coin_flips = jax.random.randint(key_list[3], (pair_count,), 0, 2)
    first_half = jnp.where(coin_flips > 0, totals - leading, leading)
    return jnp.concatenate([first_half, totals - first_half]).astype(jnp.int32)


def draw_counts(key, part):
    return brick_counts(key)


def draw_neighbors(key, part):
    counts = brick_counts(key)
    key = jax.random.fold_in(key, 202)
    key_list = jax.random.split(key, 10)
    devices = N_GZ
    slot_index = jnp.arange(CAP, dtype=jnp.int32)
    dead_slot = slot_index[None, :] >= counts[:, None]
    scores = jax.random.randint(key_list[0], (devices, CAP), 0, 1 << 20) * CAP + slot_index[None, :] + dead_slot.astype(jnp.int32) * (1 << 29)
    slot_order = jnp.argsort(scores, axis=1).astype(jnp.int32)
    rank_of = jnp.argsort(slot_order, axis=1).astype(jnp.int32)
    far_offset = jnp.full((1,), devices // 2, jnp.int32)
    offsets = jnp.concatenate([jnp.arange(1, LINKS, dtype=jnp.int32), far_offset])
    round_index = jnp.arange(LINKS, dtype=jnp.int32)
    axis_of = round_index % 3
    place_index = round_index // 3
    start_index = jnp.arange(devices, dtype=jnp.int32)
    source_device = jnp.broadcast_to(start_index[:, None], (devices, LINKS))
    dest_device = (start_index[:, None] + offsets[None, :]) % devices
    source_slot = slot_order[source_device, jnp.broadcast_to(place_index[None, :], (devices, LINKS))]
    dest_slot = slot_order[dest_device, jnp.broadcast_to(place_index[None, :], (devices, LINKS))]
    source_id = source_device * CAP + source_slot
    dest_id = dest_device * CAP + dest_slot
    valid_link = jnp.logical_not((round_index[None, :] == LINKS - 1) & (start_index[:, None] >= devices // 2))
    column_source = jnp.where(valid_link, source_id, devices * CAP)
    column_dest = jnp.where(valid_link, dest_id, devices * CAP)
    neighbor_table = jnp.full((6, devices * CAP), -1, jnp.int32)
    plus_dir = jnp.broadcast_to(2 * axis_of + 1, (devices, LINKS))
    neighbor_table = neighbor_table.at[plus_dir, column_source].set(dest_id, mode='drop')
    neighbor_table = neighbor_table.at[plus_dir - 1, column_dest].set(source_id, mode='drop')
    for axis_number in range(3):
        crossed = (LINKS - axis_number + 2) // 3
        blocked = dead_slot | (rank_of < crossed)
        score_two = jax.random.randint(key_list[3 + axis_number], (devices, CAP), 0, 1 << 20) * CAP + slot_index[None, :] + blocked.astype(jnp.int32) * (1 << 29)
        chain_order = jnp.argsort(score_two, axis=1).astype(jnp.int32)
        free_count = counts - crossed
        coin_flips = jax.random.randint(key_list[6 + axis_number], (devices, CAP - 1), 0, 4)
        linked = (coin_flips > 0) & (slot_index[None, :CAP - 1] < free_count[:, None] - 1)
        lower_id = start_index[:, None] * CAP + chain_order[:, :-1]
        upper_id = start_index[:, None] * CAP + chain_order[:, 1:]
        column_plus = jnp.where(linked, lower_id, devices * CAP)
        column_minus = jnp.where(linked, upper_id, devices * CAP)
        neighbor_table = neighbor_table.at[2 * axis_number + 1, column_plus].set(upper_id, mode='drop')
        neighbor_table = neighbor_table.at[2 * axis_number, column_minus].set(lower_id, mode='drop')
    return neighbor_table


def levels(rng, dims, shards, least, top_value):
    level, own = 1.0, jax.random.fold_in(rng, 6)
    for dim, shards_of in shards:
        draws = jnp.exp(jax.random.uniform(jax.random.fold_in(own, dim), (shards_of,), jnp.float32, least / len(shards), top_value / len(shards)))
        level = level * jnp.repeat(draws, dims[dim] // shards_of).reshape([-1 if axis == dim else 1 for axis in range(len(dims))])
    return level


def scatter_about(own_key, extent, scale, most, pieces=(), held_as=jnp.bfloat16):
    entries = jax.random.normal(own_key, extent, jnp.float32) * scale
    if len(pieces) > 0:
        entries = levels(own_key, extent, pieces, -0.22, 0.18) * entries
    return jnp.clip(entries, min=-most, max=most).astype(held_as)


def setup_inputs(seed: int = 0) -> dict:
    keys = jax.random.split(jax.random.key(seed), 10)
    features = scatter_about(keys[0], (NB, C, BR ** 3), 1.0, 6.0, ((0, 128),))
    counts = draw_counts(jax.random.fold_in(keys[9], 71), 0)
    neighbors = draw_neighbors(jax.random.fold_in(keys[9], 71), 0)
    weight_one = scatter_about(keys[3], (27, C, C), (27 * C) ** -0.5, 0.15625)
    weight_two = scatter_about(keys[4], (27, C, C), (27 * C) ** -0.5, 0.15625)
    scale_one = jnp.clip(1.0 + 0.18 * jax.random.normal(keys[5], (C,), jnp.float32), 0.1, 1.9)
    shift_one = scatter_about(keys[6], (C,), 0.5, 3.0, (), jnp.float32)
    scale_two = jnp.clip(1.0 + 0.18 * jax.random.normal(keys[7], (C,), jnp.float32), 0.1, 1.9)
    shift_two = scatter_about(keys[8], (C,), 0.5, 3.0, (), jnp.float32)
    return dict(features=features, counts=counts, neighbors=neighbors, weight_one=weight_one, weight_two=weight_two, scale_one=scale_one, shift_one=shift_one, scale_two=scale_two, shift_two=shift_two)


FLIP_ORDER = (1, 0, 3, 2, 5, 4)


def face_planes(bricks):
    amount = bricks.shape[0]
    brick_cube = bricks.reshape(amount, C, BR, BR, BR)
    plane_list = (brick_cube[:, :, 0], brick_cube[:, :, BR - 1], brick_cube[:, :, :, 0], brick_cube[:, :, :, BR - 1], brick_cube[:, :, :, :, 0], brick_cube[:, :, :, :, BR - 1])
    return jnp.stack([single.reshape(amount, C * BR * BR) for single in plane_list], axis=0)


def extend_bricks(bricks, halos):
    amount = bricks.shape[0]
    brick_cube = bricks.reshape(amount, C, BR, BR, BR)
    padded = jnp.pad(brick_cube, ((0, 0), (0, 0), (1, 1), (1, 1), (1, 1)))
    halo_sides = halos.reshape(6, amount, C, BR, BR)
    padded = padded.at[:, :, 0, 1:BR + 1, 1:BR + 1].set(halo_sides[0])
    padded = padded.at[:, :, BR + 1, 1:BR + 1, 1:BR + 1].set(halo_sides[1])
    padded = padded.at[:, :, 1:BR + 1, 0, 1:BR + 1].set(halo_sides[2])
    padded = padded.at[:, :, 1:BR + 1, BR + 1, 1:BR + 1].set(halo_sides[3])
    padded = padded.at[:, :, 1:BR + 1, 1:BR + 1, 0].set(halo_sides[4])
    padded = padded.at[:, :, 1:BR + 1, 1:BR + 1, BR + 1].set(halo_sides[5])
    return padded


def layer(bricks, neighbors, weights, scale_row, shift_row, residual, alive_rows):
    planes = face_planes(bricks)
    safe_index = jnp.clip(neighbors, 0, NB - 1)
    halos = jnp.stack([planes[FLIP_ORDER[direction]][safe_index[direction]] for direction in range(6)], axis=0)
    halos = jnp.where((neighbors >= 0)[:, :, None], halos, jnp.zeros_like(halos))
    weight_wide = weights.astype(jnp.float32)

    def one_device(packed):
        brick_part, halo_part, rest_part, live_part = packed
        padded = extend_bricks(brick_part, halo_part).astype(jnp.float32)
        result = jnp.zeros((CAP, C, BR ** 3), jnp.float32)
        for shift_x in range(3):
            stacked = jnp.stack([padded[:, :, shift_x:shift_x + BR, shift_y:shift_y + BR, shift_z:shift_z + BR].reshape(CAP, C, BR ** 3) for shift_y in range(3) for shift_z in range(3)], axis=1)
            result = result + jnp.einsum("toi,btiv->bov", weight_wide[9 * shift_x:9 * shift_x + 9], stacked, precision=lax.Precision.HIGHEST)
        values_out = result * scale_row[None, :, None] + shift_row[None, :, None]
        if rest_part is not None:
            values_out = values_out + rest_part.astype(jnp.float32)
        values_out = jnp.maximum(values_out, 0.0)
        values_out = jnp.where(live_part[:, None, None], values_out, jnp.zeros_like(values_out))
        return values_out.astype(jnp.bfloat16)

    rest_all = None if residual is None else residual.reshape(N_GZ, CAP, C, BR ** 3)
    packed = (bricks.reshape(N_GZ, CAP, C, BR ** 3), jnp.swapaxes(halos.reshape(6, N_GZ, CAP, C * BR * BR), 0, 1), rest_all, alive_rows.reshape(N_GZ, CAP))
    return lax.map(one_device, packed).reshape(NB, C, BR ** 3)


def reference(features, counts, neighbors, weight_one, weight_two, scale_one, shift_one, scale_two, shift_two):
    slot_index = jnp.arange(NB, dtype=jnp.int32)
    alive_rows = (slot_index % CAP) < counts[slot_index // CAP]
    hidden = layer(features, neighbors, weight_one, scale_one, shift_one, None, alive_rows)
    return layer(hidden, neighbors, weight_two, scale_two, shift_two, features, alive_rows)
```

```python
import functools

import jax
import jax.numpy as jnp
from jax import lax
from jax.experimental import pallas as pl
from jax.experimental.pallas import tpu as pltpu
from jax.sharding import PartitionSpec as P

C = 64
BR = 8
CAP = 32
LIVE_MAX = 30
VOX = BR**3
TAPS = 9
OFFSETS = (1, 2, 3, 4, 5, -1, -2, -3, -4, -5, 64)
PEERS = len(OFFSETS)
INVERSE = tuple(OFFSETS.index(-o) if abs(o) < 64 else PEERS - 1 for o in OFFSETS)
ZERO_SLOT = CAP
SLOTS = CAP + 1 + PEERS
F32 = jnp.float32
BF16 = jnp.bfloat16


def dot(a, b):
    return jnp.dot(a, b, preferred_element_type=F32)


def lane_of(rows):
    return lax.broadcasted_iota(jnp.int32, (rows, 128), 1)


def lane_mask(condition):
    return condition.astype(F32).astype(BF16) > 0


def roll(x, left):
    amount = (-left) % 128
    return x if amount == 0 else pltpu.roll(x, amount, 1)


def plane_voxel(k, f):
    if k < 2:
        return f + (k % 2) * 448
    if k < 4:
        return (f // 8) * 64 + f % 8 + (k % 2) * 56
    return f * 8 + (k % 2) * 7


def column(row):
    r = lax.broadcasted_iota(jnp.int32, (C, C), 0)
    c = lax.broadcasted_iota(jnp.int32, (C, C), 1)
    wide = jnp.broadcast_to(row, (C, C))
    return jnp.sum(jnp.where(r == c, wide, 0.0), axis=1, keepdims=True)


def build_weights(w_ref, wm_ref):
    for dx in range(3):
        pieces = [w_ref[9 * dx + t] for t in range(TAPS)]
        wm_ref[dx * C : (dx + 1) * C, :] = jnp.concatenate(pieces, axis=1)


def shifted(src, b, slots):
    lane = lane_of(C)
    y, z = (lane // 8) % 8, lane % 8
    n0, n1, n2, n3, n4, n5 = slots
    first = src[n1, :, 0:128]
    last = src[n0, :, 384:512]
    halo_x = jnp.where(lane_mask(lane < 64), first, last)
    zero = jnp.zeros((C, 128), BF16)
    chunks = []
    for j in range(4):
        cols = slice(128 * j, 128 * j + 128)
        own = src[b, :, cols]
        zc = {
            0: own,
            1: jnp.where(lane_mask(z == 0), roll(src[n5, :, cols], -8), own),
            -1: jnp.where(lane_mask(z == 7), roll(src[n4, :, cols], 8), own),
        }
        yn = {1: roll(src[n3, :, cols], 64), -1: roll(src[n2, :, cols], 64)}
        parts = []
        for dy in (-1, 0, 1):
            for dz in (-1, 0, 1):
                pre = zc[dz]
                if dy != 0:
                    ty = ((lane - (8 * dy + dz)) // 8) % 8
                    tz = (lane - dz) % 8
                    edge = ty == (7 if dy > 0 else 0)
                    beyond = tz == (7 if dz > 0 else 0)
                    pre = jnp.where(lane_mask(edge), yn[dy], pre)
                    if dz != 0:
                        pre = jnp.where(lane_mask(edge & beyond), zero, pre)
                parts.append(roll(pre, 8 * dy + dz))
        chunks.append(jnp.concatenate(parts, axis=0))
    parts = []
    for dy in (-1, 0, 1):
        for dz in (-1, 0, 1):
            sy, sz = y - dy, z - dz
            inside = (sy >= 0) & (sy < 8) & (sz >= 0) & (sz < 8)
            pre = halo_x
            if dy != 0 or dz != 0:
                pre = jnp.where(lane_mask(inside), pre, zero)
            parts.append(roll(pre, 8 * dy + dz))
    chunks.append(jnp.concatenate(parts, axis=0))
    return chunks


def combine(products):
    lane = lane_of(C)
    low = lane < 64
    y0 = [p[0:C] for p in products]
    y1 = [p[C : 2 * C] for p in products]
    y2 = [p[2 * C : 3 * C] for p in products]
    before = [y0[4], y0[0], y0[1], y0[2], y0[3]]
    sums = [y2[j] + before[j] for j in range(5)]
    return [y1[j] + roll(jnp.where(low, sums[j + 1], sums[j]), 64) for j in range(4)]


def kernel(
    feat_ref, counts_ref, nbr_ref, nbv_ref, w1_ref, w2_ref, s1_ref, t1_ref, s2_ref, t2_ref,
    out_ref,
    xb, hb, wm, z_buf, pack_tab, open_tab, affine, send_buf, recv_buf,
    load_sem, send_sem, recv_sem,
):
    devices = lax.axis_size("gz")
    me = lax.axis_index("gz")
    load = pltpu.make_async_copy(feat_ref, xb.at[pl.ds(0, CAP)], load_sem)
    load.start()
    peers = [lax.rem(me + (o + devices), devices) for o in OFFSETS]
    barrier = pltpu.get_barrier_semaphore()
    for peer in peers:
        pl.semaphore_signal(
            barrier, inc=1, device_id=(peer,), device_id_type=pl.DeviceIdType.MESH
        )

    zero_brick = jnp.zeros((C, VOX), BF16)
    xb[ZERO_SLOT] = zero_brick
    hb[ZERO_SLOT] = zero_brick
    build_weights(w1_ref, wm)
    for i, ref in enumerate((s1_ref, t1_ref, s2_ref, t2_ref)):
        affine[i] = jnp.broadcast_to(column(ref[...]), (C, 128))
    for k in range(6):
        rows = lax.broadcasted_iota(jnp.int32, (VOX, 128), 0)
        f = lax.broadcasted_iota(jnp.int32, (VOX, 128), 1) % 64
        pack_tab[k] = (rows == plane_voxel(k, f)).astype(F32).astype(BF16)
        f = lax.broadcasted_iota(jnp.int32, (128, VOX), 0) % 64
        cols = lax.broadcasted_iota(jnp.int32, (128, VOX), 1)
        open_tab[k] = (cols == plane_voxel(k, f)).astype(F32).astype(BF16)

    nbv = nbv_ref[...]
    distance = lax.rem((nbv // CAP) - me + 2 * devices, devices)
    entry = lax.broadcasted_iota(jnp.int32, nbv.shape, 0) * CAP + lax.broadcasted_iota(
        jnp.int32, nbv.shape, 1
    )
    face_k, face_b = [], []
    for o in OFFSETS:
        hit = (nbv >= 0) & (distance == o % 128)
        where = jnp.minimum(jnp.sum(jnp.where(hit, entry, 0)), 6 * CAP - 1)
        face_k.append(where // CAP)
        face_b.append(where % CAP)

    def slot_of(k, b):
        nb = nbr_ref[k, b]
        owner = nb // CAP
        dist = lax.rem(owner - me + 2 * devices, devices)
        far = jnp.where(
            dist == 64,
            PEERS - 1,
            jnp.where(dist <= 5, dist - 1, 4 + devices - dist),
        )
        slot = jnp.where(dist == 0, nb % CAP, CAP + 1 + far)
        return jnp.clip(jnp.where(nb < 0, ZERO_SLOT, slot), 0, SLOTS - 1)

    def pack_and_send(src, phase):
        low = lane_mask(lane_of(32) < 64)
        copies = []
        for p in range(PEERS):
            face = dot(src[face_b[p]], pack_tab[face_k[p]]).astype(BF16)
            send_buf[phase, p] = jnp.where(low, face[0:32], face[32:64])
        for p in range(PEERS):
            copy = pltpu.make_async_remote_copy(
                src_ref=send_buf.at[phase, p],
                dst_ref=recv_buf.at[phase, INVERSE[p]],
                send_sem=send_sem.at[phase, p],
                recv_sem=recv_sem.at[phase, INVERSE[p]],
                device_id=(peers[p],),
                device_id_type=pl.DeviceIdType.MESH,
            )
            copy.start()
            copies.append(copy)
        return copies

    def receive(dst, phase, copies):
        low = lane_mask(lane_of(32) < 64)
        zero = jnp.zeros((32, 128), BF16)
        for copy in copies:
            copy.wait()
        for p in range(PEERS):
            got = recv_buf[phase, p]
            face = jnp.concatenate([jnp.where(low, got, zero), jnp.where(low, zero, got)], axis=0)
            k = face_k[p]
            flip = k + 1 - 2 * (k % 2)
            dst[CAP + 1 + p] = dot(face, open_tab[flip]).astype(BF16)

    count = counts_ref[0]

    def convolve(src, scale, shift, store):
        def body(i, carry):
            bricks = [2 * i, 2 * i + 1]
            chunks = []
            for b in bricks:
                chunks += shifted(src, b, [slot_of(k, b) for k in range(6)])
            z_buf[...] = jnp.concatenate(chunks, axis=1)
            product = dot(wm[...], z_buf[...])
            blocks = [product[:, 128 * j : 128 * j + 128] for j in range(10)]
            for n, b in enumerate(bricks):
                live = b < count
                for j, value in enumerate(combine(blocks[5 * n : 5 * n + 5])):
                    store(b, slice(128 * j, 128 * j + 128), value * scale + shift, live)
            return carry

        lax.fori_loop(0, LIVE_MAX // 2, body, 0)

    def store_hidden(b, cols, value, live):
        value = jnp.maximum(value, 0.0)
        hb[b, :, cols] = jnp.where(live, value, jnp.zeros_like(value)).astype(BF16)

    def store_out(b, cols, value, live):
        value = jnp.maximum(value + xb[b, :, cols].astype(F32), 0.0)
        out_ref[b, :, cols] = jnp.where(live, value, jnp.zeros_like(value)).astype(BF16)

    load.wait()
    pl.semaphore_wait(barrier, PEERS)
    copies = pack_and_send(xb, 0)
    receive(xb, 0, copies)
    convolve(xb, affine[0], affine[1], store_hidden)
    copies = pack_and_send(hb, 1)
    build_weights(w2_ref, wm)
    receive(hb, 1, copies)
    convolve(hb, affine[2], affine[3], store_out)
    for b in range(LIVE_MAX, CAP):
        out_ref[b] = zero_brick


def on_device(
    features, counts, neighbors, weight_one, weight_two, scale_one, shift_one, scale_two, shift_two
):
    vmem = pl.BlockSpec(memory_space=pltpu.VMEM)
    smem = pl.BlockSpec(memory_space=pltpu.SMEM)
    rows = [v.reshape(1, C) for v in (scale_one, shift_one, scale_two, shift_two)]
    return pl.pallas_call(
        kernel,
        out_shape=jax.ShapeDtypeStruct((CAP, C, VOX), BF16),
        in_specs=[pl.BlockSpec(memory_space=pltpu.HBM), smem, smem] + [vmem] * 7,
        out_specs=vmem,
        scratch_shapes=[
            pltpu.VMEM((SLOTS, C, VOX), BF16),
            pltpu.VMEM((SLOTS, C, VOX), BF16),
            pltpu.VMEM((3 * C, TAPS * C), BF16),
            pltpu.VMEM((TAPS * C, 1280), BF16),
            pltpu.VMEM((6, VOX, 128), BF16),
            pltpu.VMEM((6, 128, VOX), BF16),
            pltpu.VMEM((4, C, 128), F32),
            pltpu.VMEM((2, PEERS, 32, 128), BF16),
            pltpu.VMEM((2, PEERS, 32, 128), BF16),
            pltpu.SemaphoreType.DMA,
            pltpu.SemaphoreType.DMA((2, PEERS)),
            pltpu.SemaphoreType.DMA((2, PEERS)),
        ],
        compiler_params=pltpu.CompilerParams(
            collective_id=0, has_side_effects=True, vmem_limit_bytes=40 << 20
        ),
    )(features, counts, neighbors, neighbors, weight_one, weight_two, *rows)


def solution(mesh):
    in_specs = (P("gz", None, None), P("gz"), P(None, "gz"), P(), P(), P(), P(), P(), P())
    out_specs = P("gz", None, None)
    return jax.shard_map(
        on_device, mesh=mesh, in_specs=in_specs, out_specs=out_specs, check_vma=False
    )
```

```python
import jax
import jax.numpy as jnp
from jax import lax
from jax.experimental import pallas as pl
from jax.experimental.pallas import tpu as pltpu
from jax.sharding import PartitionSpec as P

C = 64
BR = 8
CAP = 32
HALF = CAP // 2
VOX = BR**3
LANES = CAP * BR
PARK = 30 * BR
ROWS = 3 * C
OFFSETS = (1, 2, 3, 4, 5, -1, -2, -3, -4, -5, 64)
PEERS = len(OFFSETS)
INVERSE = tuple(OFFSETS.index(-o) if abs(o) < 64 else PEERS - 1 for o in OFFSETS)
F32 = jnp.float32
BF16 = jnp.bfloat16


def dot(a, b):
    return jnp.dot(a, b, preferred_element_type=F32)


def dot_nt(a, b):
    return lax.dot_general(a, b, (((1,), (1,)), ((), ())), preferred_element_type=F32)


def iota(shape, dim):
    return lax.broadcasted_iota(jnp.int32, shape, dim)


def one_hot(condition):
    return jnp.where(condition, 1.0, 0.0).astype(BF16)


def column(row):
    wide = jnp.broadcast_to(row, (C, C))
    return jnp.sum(jnp.where(iota((C, C), 0) == iota((C, C), 1), wide, 0.0), axis=1, keepdims=True)


def center(x, y):
    return x + 1, pl.ds(ROWS * (y + 1) + C, C)


def kernel(
    feat_hbm, counts_ref, nbr_hbm, w1_hbm, w2_hbm, s1_hbm, t1_hbm, s2_hbm, t2_hbm,
    act_hbm,
    feat, nbv, w_raw, rows, z1, z2, wa, wb, affine, regroup, act,
    g_near, g_far, g_send, g_shift, g_inner, send_buf, recv_buf, unpack, remote,
    load_sem, send_sem, recv_sem, save_sem,
):
    devices = lax.axis_size("gz")
    me = lax.axis_index("gz")
    loads = [
        pltpu.make_async_copy(feat_hbm, feat, load_sem.at[0]),
        pltpu.make_async_copy(nbr_hbm, nbv, load_sem.at[1]),
        pltpu.make_async_copy(w1_hbm, w_raw.at[0], load_sem.at[2]),
        pltpu.make_async_copy(w2_hbm, w_raw.at[1], load_sem.at[3]),
    ]
    for i, ref in enumerate((s1_hbm, t1_hbm, s2_hbm, t2_hbm)):
        loads.append(pltpu.make_async_copy(ref, rows.at[i], load_sem.at[4 + i]))
    for load in loads:
        load.start()
    peers = [lax.rem(me + (o + devices), devices) for o in OFFSETS]
    barrier = pltpu.get_barrier_semaphore()
    for peer in peers:
        pl.semaphore_signal(
            barrier, inc=1, device_id=(peer,), device_id_type=pl.DeviceIdType.MESH
        )

    corner = jnp.zeros((ROWS, LANES), BF16)
    for z in (z1, z2):
        for x in (0, BR + 1):
            for y in (0, BR + 1):
                z[x, ROWS * y : ROWS * y + ROWS, :] = corner
    recv_buf[:, PEERS:] = jnp.zeros((2, 16 - PEERS, 16, 256), BF16)

    loads[1].wait()
    table = jnp.concatenate([nbv[...], jnp.full((2, CAP), -1, jnp.int32)], axis=0)
    dist = ((table >> 5) - me + 2 * devices) & (devices - 1)
    peer_at = jnp.where(dist == 64, PEERS - 1, jnp.where(dist <= 5, dist - 1, 132 - dist))
    code = jnp.where(dist == 0, table & (CAP - 1), CAP + peer_at)
    code = jnp.where(table < 0, -1, code).astype(F32).astype(BF16)
    widen = one_hot(iota((CAP, LANES), 0) == iota((CAP, LANES), 1) >> 3)
    wide = dot(code, widen).astype(jnp.int32) * 8
    lane_z = iota((1, LANES), 1) & 7
    wide = [jnp.where(wide[k : k + 1] < 0, -4096, wide[k : k + 1]) for k in range(6)]
    peer = [(wide[k] >> 3) - CAP for k in range(6)]
    lane = iota((1, LANES), 1)
    row_near = iota((LANES, LANES), 0)
    row_far = iota((128, LANES), 0)
    low_edge, high_edge = lane_z == 0, lane_z == 7
    for k in range(4):
        g_near[k] = one_hot(row_near == jnp.where(peer[k] < 0, wide[k] + lane_z, -1))
        g_far[k] = one_hot(row_far == jnp.where(peer[k] < 0, -1, 16 * lane_z + peer[k]))
        g_send[k] = one_hot(row_far == jnp.where(peer[k] < 0, -1, 8 * peer[k] + lane_z))
    below = jnp.where(peer[4] < 0, wide[4] + 7, PARK + peer[4])
    above = jnp.where(peer[5] < 0, wide[5], PARK + peer[5])
    g_shift[:, 0:LANES] = one_hot(row_near == jnp.where(low_edge, below, lane - 1))
    g_shift[:, LANES:] = one_hot(row_near == jnp.where(high_edge, above, lane + 1))
    inner = one_hot(row_near == jnp.where(low_edge, -1, lane - 1))
    g_inner[:, 0:LANES] = inner
    g_inner[:, LANES:] = one_hot(row_near == jnp.where(high_edge, -1, lane + 1))
    for y in range(BR):
        key = jnp.where(high_edge, peer[5], jnp.where(low_edge, peer[4], -1))
        g_send[4 + y] = one_hot(row_far == jnp.where(key < 0, -1, 8 * key + y))

    for load in loads[2:]:
        load.wait()
    for n in range(2):
        for dy in range(3):
            pieces = [w_raw[n, 9 * (t // 3) + 3 * dy + t % 3] for t in range(8)]
            wa[n, dy * C : dy * C + C, :] = jnp.concatenate(pieces, axis=1)
        wb[n] = jnp.concatenate([w_raw[n, 20 + 3 * dy] for dy in range(3)], axis=1)
    for i in range(4):
        affine[i] = jnp.broadcast_to(column(rows[i : i + 1, :]), (C, LANES))
    loads[0].wait()

    def enter(j, carry):
        cols = pl.ds(pl.multiple_of(128 * j, 128), 128)
        for p in range(HALF):
            both = jnp.concatenate([feat[p, :, cols], feat[p + HALF, :, cols]], axis=0)
            regroup[:, p] = both.T.astype(F32).reshape(HALF, 8, 128)
        for n in range(16):
            both = regroup[n].reshape(128, 128).astype(BF16).T
            x, at = center(2 * j + n // 8, n % 8)
            z1[x, at, 0:128] = both[0:C]
            z1[x, at, 128:256] = both[C:]
        return carry

    lax.fori_loop(0, 4, enter, 0)
    pl.semaphore_wait(barrier, PEERS)

    def layer_x(z, x):
        return jnp.concatenate([z[center(x, y)] for y in range(BR)], axis=0)

    def layer_y(z, y):
        return jnp.concatenate([z[center(x, y)] for x in range(BR)], axis=0)

    def exchange(z, phase):
        picked = jnp.zeros((8 * C, 128), F32)
        faces = [layer_x(z, 0), layer_x(z, 7), layer_y(z, 0), layer_y(z, 7)]
        for k in range(4):
            picked = picked + dot_nt(faces[k], g_send[k])
        for y in range(BR):
            picked = picked + dot_nt(layer_y(z, y), g_send[4 + y])
        picked = picked.astype(BF16)
        blocks = [
            picked[128 * i : 128 * i + 128].T.astype(F32).reshape(16, 8, 128) for i in range(4)
        ]
        for i in range(2):
            pair = jnp.concatenate([blocks[2 * i], blocks[2 * i + 1]], axis=1).astype(BF16)
            send_buf[phase, :, :, 128 * i : 128 * i + 128] = pair
        copies = []
        for p in range(PEERS):
            copy = pltpu.make_async_remote_copy(
                src_ref=send_buf.at[phase, p],
                dst_ref=recv_buf.at[phase, INVERSE[p]],
                send_sem=send_sem.at[phase, p],
                recv_sem=recv_sem.at[phase, INVERSE[p]],
                device_id=(peers[p],),
                device_id_type=pl.DeviceIdType.MESH,
            )
            copy.start()
            copies.append(copy)
        for copy in copies:
            copy.wait()
        for i in range(2):
            pair = recv_buf[phase, :, :, 128 * i : 128 * i + 128].astype(F32)
            for h in range(2):
                unpack[2 * i + h] = pair[:, 8 * h : 8 * h + 8].reshape(128, 128)
        parked = iota((16, 128), 1) >= PARK - 128
        parked = jnp.concatenate([one_hot(parked)] * 8, axis=0) > 0
        for i in range(4):
            block = jnp.concatenate(
                [unpack[i, pl.ds(q, 16, stride=8), :] for q in range(BR)], axis=0
            )
            block = block.astype(BF16).T
            remote[128 * i : 128 * i + 128, :] = block
            for q in range(BR):
                shifted = pltpu.roll(block, PARK - 128 - 16 * q, 1) if q < 7 else block
                both = jnp.concatenate([z[center(2 * i + n, q)][:, 128:] for n in range(2)], axis=0)
                both = jnp.where(parked, shifted, both)
                for n in range(2):
                    x, at = center(2 * i + n, q)
                    z[x, at, 128:] = both[C * n : C * n + C]

    def fill(z):
        for k in range(4):
            face = layer_x(z, 7 - 7 * k) if k < 2 else layer_y(z, 7 - 7 * (k - 2))
            halo = dot(face, g_near[k]) + dot(remote[...], g_far[k])
            halo = halo.astype(BF16)
            sides = dot(halo, g_inner[...]).astype(BF16)
            for a in range(BR):
                if k < 2:
                    x, base = (BR + 1) * k, ROWS * (a + 1)
                else:
                    x, base = a + 1, ROWS * (BR + 1) * (k - 2)
                rows = slice(C * a, C * a + C)
                z[x, base : base + C, :] = sides[rows, 0:LANES]
                z[x, base + C : base + 2 * C, :] = halo[rows]
                z[x, base + 2 * C : base + 3 * C, :] = sides[rows, LANES:]

        def edges(y, carry):
            sides = dot(layer_y(z, y), g_shift[...]).astype(BF16)
            base = ROWS * (y + 1)
            for x in range(BR):
                z[x + 1, pl.ds(base, C), :] = sides[C * x : C * x + C, 0:LANES]
                z[x + 1, pl.ds(base + 2 * C, C), :] = sides[C * x : C * x + C, LANES:]
            return carry

        lax.fori_loop(0, BR, edges, 0)

    alive = (iota((C, LANES), 1) >> 3) < counts_ref[0]

    def convolve(z, n, store, done):
        def body(x, carry):
            products = []
            for y in range(BR + 2):
                at = slice(ROWS * y, ROWS * y + ROWS)
                stack = jnp.concatenate(
                    [z[x, at, :], z[x + 1, at, :], z[x + 2, ROWS * y : ROWS * y + 2 * C, :]], axis=0
                )
                if y == 0:
                    lhs = wa[n, 0:C]
                elif y == BR + 1:
                    lhs = wa[n, 2 * C :]
                else:
                    lhs = wa[n]
                products.append(dot(lhs, stack))
            for y in range(BR):
                last = jnp.concatenate(
                    [z[x + 2, ROWS * (y + d) + 2 * C : ROWS * (y + d) + 3 * C, :] for d in range(3)],
                    axis=0,
                )
                total = products[y][0:C] + products[y + 1][C : 2 * C]
                top = products[y + 2]
                total = total + (top if y == BR - 1 else top[2 * C :])
                total = total + dot(wb[n], last)
                store(x, y, total * affine[2 * n] + affine[2 * n + 1])
            done(x)
            return carry

        lax.fori_loop(0, BR, body, 0)

    def store_hidden(x, y, value):
        value = jnp.where(alive, jnp.maximum(value, 0.0), 0.0)
        z2[center(x, y)] = value.astype(BF16)

    def store_out(x, y, value):
        value = jnp.maximum(value + z1[center(x, y)].astype(F32), 0.0)
        act[x, y] = jnp.where(alive, value, 0.0).astype(BF16)

    def saving(x):
        return pltpu.make_async_copy(act.at[x], act_hbm.at[x], save_sem.at[x])

    exchange(z1, 0)
    fill(z1)
    convolve(z1, 0, store_hidden, lambda x: None)
    exchange(z2, 1)
    fill(z2)
    convolve(z2, 1, store_out, lambda x: saving(x).start())

    for x in range(BR):
        saving(x).wait()


def leave(act_ref, out_ref, spread):
    for n in range(16):
        value = act_ref[n // 8, n % 8]
        both = jnp.concatenate([value[:, 0:128], value[:, 128:256]], axis=0).T
        spread[:, n] = both.astype(F32).reshape(HALF, 8, 128)
    for p in range(HALF):
        both = spread[p].reshape(128, 128).astype(BF16).T
        out_ref[p] = both[0:C]
        out_ref[p + HALF] = both[C:]


def on_device(
    features, counts, neighbors, weight_one, weight_two, scale_one, shift_one, scale_two, shift_two
):
    hbm = pl.BlockSpec(memory_space=pltpu.HBM)
    smem = pl.BlockSpec(memory_space=pltpu.SMEM)
    act = pl.pallas_call(
        kernel,
        out_shape=jax.ShapeDtypeStruct((BR, BR, C, LANES), BF16),
        in_specs=[hbm, smem] + [hbm] * 7,
        out_specs=hbm,
        scratch_shapes=[
            pltpu.VMEM((CAP, C, VOX), BF16),
            pltpu.VMEM((6, CAP), jnp.int32),
            pltpu.VMEM((2, 27, C, C), BF16),
            pltpu.VMEM((4, C), F32),
            pltpu.VMEM((BR + 2, ROWS * (BR + 2), LANES), BF16),
            pltpu.VMEM((BR + 2, ROWS * (BR + 2), LANES), BF16),
            pltpu.VMEM((2, 3 * C, 8 * C), BF16),
            pltpu.VMEM((2, C, 3 * C), BF16),
            pltpu.VMEM((4, C, LANES), F32),
            pltpu.VMEM((16, HALF, 8, 128), F32),
            pltpu.VMEM((BR, BR, C, LANES), BF16),
            pltpu.VMEM((4, LANES, LANES), BF16),
            pltpu.VMEM((4, 128, LANES), BF16),
            pltpu.VMEM((12, 128, LANES), BF16),
            pltpu.VMEM((LANES, 2 * LANES), BF16),
            pltpu.VMEM((LANES, 2 * LANES), BF16),
            pltpu.VMEM((2, 16, 16, 256), BF16),
            pltpu.VMEM((2, 16, 16, 256), BF16),
            pltpu.VMEM((4, 128, 128), F32),
            pltpu.VMEM((8 * C, 128), BF16),
            pltpu.SemaphoreType.DMA((8,)),
            pltpu.SemaphoreType.DMA((2, PEERS)),
            pltpu.SemaphoreType.DMA((2, PEERS)),
            pltpu.SemaphoreType.DMA((BR,)),
        ],
        compiler_params=pltpu.CompilerParams(
            collective_id=0, has_side_effects=True, vmem_limit_bytes=61 << 20
        ),
    )(
        features, counts, neighbors, weight_one, weight_two,
        scale_one, shift_one, scale_two, shift_two,
    )
    return pl.pallas_call(
        leave,
        grid=(4,),
        out_shape=jax.ShapeDtypeStruct((CAP, C, VOX), BF16),
        in_specs=[pl.BlockSpec((2, BR, C, LANES), lambda j: (j, 0, 0, 0))],
        out_specs=pl.BlockSpec((CAP, C, 128), lambda j: (0, 0, j)),
        scratch_shapes=[pltpu.VMEM((HALF, 16, 8, 128), F32)],
        compiler_params=pltpu.CompilerParams(vmem_limit_bytes=60 << 20),
    )(act)


def solution(mesh):
    in_specs = (P("gz", None, None), P("gz"), P(None, "gz"), P(), P(), P(), P(), P(), P())
    out_specs = P("gz", None, None)
    return jax.shard_map(
        on_device, mesh=mesh, in_specs=in_specs, out_specs=out_specs, check_vma=False
    )
```

```python
import jax
import jax.numpy as jnp
from jax import lax
from jax.experimental import pallas as pl
from jax.experimental.pallas import tpu as pltpu
from jax.sharding import PartitionSpec as P

C = 64
BR = 8
CAP = 32
HALF = CAP // 2
VOX = BR**3
LANES = CAP * BR
PARKED_SLOT = 30
PARK = PARKED_SLOT * BR
ROWS = 3 * C
OFFSETS = (1, 2, 3, 4, 5, -1, -2, -3, -4, -5, 64)
PEERS = len(OFFSETS)
INVERSE = tuple(OFFSETS.index(-o) if abs(o) < 64 else PEERS - 1 for o in OFFSETS)
F32 = jnp.float32
BF16 = jnp.bfloat16


def dot(a, b):
    return jnp.dot(a, b, preferred_element_type=F32)


def dot_nt(a, b):
    return lax.dot_general(a, b, (((1,), (1,)), ((), ())), preferred_element_type=F32)


def iota(shape, dim):
    return lax.broadcasted_iota(jnp.int32, shape, dim)


def one_hot(condition):
    return jnp.where(condition, 1.0, 0.0).astype(BF16)


def column(row):
    wide = jnp.broadcast_to(row, (C, C))
    return jnp.sum(jnp.where(iota((C, C), 0) == iota((C, C), 1), wide, 0.0), axis=1, keepdims=True)


def center(x, y):
    return x + 1, pl.ds(ROWS * (y + 1) + C, C)


def kernel(
    feat_hbm, counts_ref, nbr_hbm, w1_hbm, w2_hbm, s1_hbm, t1_hbm, s2_hbm, t2_hbm,
    act_hbm, order_ref,
    feat, nbv, w_raw, rows, z1, z2, wa, wb, affine, alive, regroup, act,
    g_near, g_far, g_send, g_shift, g_inner, send_buf, recv_buf, unpack, remote,
    load_sem, send_sem, recv_sem, save_sem,
):
    devices = lax.axis_size("gz")
    me = lax.axis_index("gz")
    loads = [
        pltpu.make_async_copy(feat_hbm, feat, load_sem.at[0]),
        pltpu.make_async_copy(nbr_hbm, nbv, load_sem.at[1]),
        pltpu.make_async_copy(w1_hbm, w_raw.at[0], load_sem.at[2]),
        pltpu.make_async_copy(w2_hbm, w_raw.at[1], load_sem.at[3]),
    ]
    for i, ref in enumerate((s1_hbm, t1_hbm, s2_hbm, t2_hbm)):
        loads.append(pltpu.make_async_copy(ref, rows.at[i], load_sem.at[4 + i]))
    for load in loads:
        load.start()
    peers = [lax.rem(me + (o + devices), devices) for o in OFFSETS]
    barrier = pltpu.get_barrier_semaphore()
    for peer in peers:
        pl.semaphore_signal(
            barrier, inc=1, device_id=(peer,), device_id_type=pl.DeviceIdType.MESH
        )

    corner = jnp.zeros((ROWS, 128), BF16)
    for z in (z1, z2):
        for g in range(2):
            for x in (0, BR + 1):
                for y in (0, BR + 1):
                    z[g, x, ROWS * y : ROWS * y + ROWS, :] = corner
    recv_buf[:, PEERS:] = jnp.zeros((2, 16 - PEERS, 16, 256), BF16)

    loads[1].wait()
    table = nbv[...]
    dist = ((table >> 5) - me + 2 * devices) & (devices - 1)
    peer_at = jnp.where(dist == 64, PEERS - 1, jnp.where(dist <= 5, dist - 1, 132 - dist))
    borders = jnp.where((table >= 0) & (dist != 0), 1.0, 0.0)
    borders = jnp.max(borders, axis=0, keepdims=True)
    slot = iota((1, CAP), 1)
    usable = slot < PARKED_SLOT
    flags = jnp.concatenate(
        [jnp.where(usable, borders, 0.0), jnp.where(usable, 1.0 - borders, 0.0)]
        + [jnp.zeros((6, CAP), F32)], axis=0,
    ).astype(BF16)
    ranks = dot(flags, one_hot(iota((CAP, CAP), 0) < iota((CAP, CAP), 1)))
    plain = jnp.sum(flags[1:2].astype(F32), axis=1, keepdims=True)
    place = jnp.where(borders > 0.5, plain + ranks[0:1], ranks[1:2])
    place = jnp.where(usable, place.astype(jnp.int32), slot)
    square = iota((CAP, CAP), 0) == iota((CAP, CAP), 1)
    place_column = jnp.sum(
        jnp.where(square, jnp.broadcast_to(place, (CAP, CAP)), 0), axis=1, keepdims=True
    )
    order = [jnp.sum(jnp.where(place == s, slot, 0)) for s in range(CAP)]
    order = [jnp.clip(s, 0, CAP - 1) for s in order]
    for s in range(CAP):
        order_ref[s] = order[s]

    codes = []
    for k in range(6):
        local = jnp.where(iota((CAP, CAP), 0) == (table[k : k + 1] & (CAP - 1)), place_column, 0)
        local = jnp.sum(local, axis=0, keepdims=True)
        code = jnp.where(dist[k : k + 1] == 0, local, CAP + peer_at[k : k + 1])
        codes.append(jnp.where(table[k : k + 1] < 0, -1, code))
    codes.append((slot < counts_ref[0]).astype(jnp.int32))
    codes.append(jnp.zeros((1, CAP), jnp.int32))
    codes = jnp.concatenate(codes, axis=0).astype(F32).astype(BF16)
    wide = dot(codes, one_hot(place_column == iota((CAP, LANES), 1) >> 3)).astype(jnp.int32)
    alive_row = wide[6:7]
    wide = [jnp.where(wide[k : k + 1] < 0, -4096, wide[k : k + 1] * 8) for k in range(6)]
    peer = [(wide[k] >> 3) - CAP for k in range(6)]
    lane = iota((1, LANES), 1)
    lane_z = lane & 7
    row_near = iota((LANES, LANES), 0)
    row_far = iota((128, 128), 0)
    low_edge, high_edge = lane_z == 0, lane_z == 7
    for k in range(4):
        g_near[k] = one_hot(row_near == jnp.where(peer[k] < 0, wide[k] + lane_z, -1))
        far = peer[k][:, 128:]
        z_far = lane_z[:, 128:]
        g_far[k] = one_hot(row_far == jnp.where(far < 0, -1, 16 * z_far + far))
        g_send[k] = one_hot(row_far == jnp.where(far < 0, -1, 8 * far + z_far))
    below = jnp.where(peer[4] < 0, wide[4] + 7, PARK + peer[4])
    above = jnp.where(peer[5] < 0, wide[5], PARK + peer[5])
    before = one_hot(row_near == jnp.where(low_edge, below, lane - 1))
    after = one_hot(row_near == jnp.where(high_edge, above, lane + 1))
    for g in range(2):
        cols = slice(128 * g, 128 * g + 128)
        g_shift[g] = jnp.concatenate([before[:, cols], after[:, cols]], axis=1)
    lane, edge = lane[:, 0:128], lane_z[:, 0:128]
    g_inner[:, 0:128] = one_hot(row_far == jnp.where(edge == 0, -1, lane - 1))
    g_inner[:, 128:] = one_hot(row_far == jnp.where(edge == 7, -1, lane + 1))
    for y in range(BR):
        key = jnp.where(high_edge, peer[5], jnp.where(low_edge, peer[4], -1))[:, 128:]
        g_send[4 + y] = one_hot(row_far == jnp.where(key < 0, -1, 8 * key + y))
    for i in range(2):
        alive[i] = jnp.broadcast_to(alive_row[:, 128 * i : 128 * i + 128], (8, 128)).astype(F32)

    for load in loads[2:]:
        load.wait()
    for n in range(2):
        for dy in range(3):
            pieces = [w_raw[n, 9 * (t // 3) + 3 * dy + t % 3] for t in range(8)]
            wa[n, dy * C : dy * C + C, :] = jnp.concatenate(pieces, axis=1)
        wb[n] = jnp.concatenate([w_raw[n, 20 + 3 * dy] for dy in range(3)], axis=1)
    for i in range(4):
        affine[i] = jnp.broadcast_to(column(rows[i : i + 1, :]), (C, 128))
    loads[0].wait()

    def enter(j, carry):
        cols = pl.ds(pl.multiple_of(128 * j, 128), 128)
        for p in range(HALF):
            both = jnp.concatenate([feat[order[p], :, cols], feat[order[p + HALF], :, cols]], axis=0)
            regroup[:, p] = both.T.astype(F32).reshape(HALF, 8, 128)
        for n in range(16):
            both = regroup[n].reshape(128, 128).astype(BF16).T
            x, at = center(2 * j + n // 8, n % 8)
            z1[0, x, at, :] = both[0:C]
            z1[1, x, at, :] = both[C:]
        return carry

    lax.fori_loop(0, 4, enter, 0)

    def block(z, g, x, y):
        return z[(g,) + center(x, y)]

    def both_groups(z, x, y):
        return jnp.concatenate([block(z, 0, x, y), block(z, 1, x, y)], axis=1)

    def layer(read, x=None, y=None):
        at = [(x, i) if y is None else (i, y) for i in range(BR)]
        return jnp.concatenate([read(*i) for i in at], axis=0)

    def send(z, phase):
        def read(x, y):
            return block(z, 1, x, y)

        faces = [layer(read, x=0), layer(read, x=7), layer(read, y=0), layer(read, y=7)]
        faces += [layer(read, y=y) for y in range(BR)]
        picked = jnp.zeros((8 * C, 128), F32)
        for k in range(12):
            picked = picked + dot_nt(faces[k], g_send[k])
        picked = picked.astype(BF16)
        blocks = [
            picked[128 * i : 128 * i + 128].T.astype(F32).reshape(16, 8, 128) for i in range(4)
        ]
        for i in range(2):
            pair = jnp.concatenate([blocks[2 * i], blocks[2 * i + 1]], axis=1).astype(BF16)
            send_buf[phase, :, :, 128 * i : 128 * i + 128] = pair
        if phase == 0:
            pl.semaphore_wait(barrier, PEERS)
        copies = []
        for p in range(PEERS):
            copy = pltpu.make_async_remote_copy(
                src_ref=send_buf.at[phase, p],
                dst_ref=recv_buf.at[phase, INVERSE[p]],
                send_sem=send_sem.at[phase, p],
                recv_sem=recv_sem.at[phase, INVERSE[p]],
                device_id=(peers[p],),
                device_id_type=pl.DeviceIdType.MESH,
            )
            copy.start()
            copies.append(copy)
        return copies

    def receive(z, phase, copies):
        for copy in copies:
            copy.wait()
        for i in range(2):
            pair = recv_buf[phase, :, :, 128 * i : 128 * i + 128].astype(F32)
            for h in range(2):
                unpack[2 * i + h] = pair[:, 8 * h : 8 * h + 8].reshape(128, 128)
        parked = one_hot(iota((16, 128), 1) >= PARK - 128)
        parked = jnp.concatenate([parked] * 8, axis=0) > 0
        for i in range(4):
            got = jnp.concatenate(
                [unpack[i, pl.ds(q, 16, stride=8), :] for q in range(BR)], axis=0
            )
            got = got.astype(BF16).T
            remote[128 * i : 128 * i + 128, :] = got
            for q in range(BR):
                shifted = pltpu.roll(got, PARK - 128 - 16 * q, 1) if q < 7 else got
                both = jnp.concatenate([block(z, 1, 2 * i + n, q) for n in range(2)], axis=0)
                both = jnp.where(parked, shifted, both)
                for n in range(2):
                    z[(1,) + center(2 * i + n, q)] = both[C * n : C * n + C]

    def fill(z, g):
        def read(x, y):
            return both_groups(z, x, y)

        cols = slice(128 * g, 128 * g + 128)
        for k in range(4):
            face = layer(read, x=7 - 7 * k) if k < 2 else layer(read, y=7 - 7 * (k - 2))
            halo = dot(face, g_near[k, :, cols])
            if g == 1:
                halo = halo + dot(remote[...], g_far[k])
            halo = halo.astype(BF16)
            sides = dot(halo, g_inner[...]).astype(BF16)
            for a in range(BR):
                if k < 2:
                    x, base = (BR + 1) * k, ROWS * (a + 1)
                else:
                    x, base = a + 1, ROWS * (BR + 1) * (k - 2)
                rows = slice(C * a, C * a + C)
                z[g, x, base : base + C, :] = sides[rows, 0:128]
                z[g, x, base + C : base + 2 * C, :] = halo[rows]
                z[g, x, base + 2 * C : base + 3 * C, :] = sides[rows, 128:]

        def edges(y, carry):
            sides = dot(layer(read, y=y), g_shift[g]).astype(BF16)
            base = ROWS * (y + 1)
            for x in range(BR):
                z[g, x + 1, pl.ds(base, C), :] = sides[C * x : C * x + C, 0:128]
                z[g, x + 1, pl.ds(base + 2 * C, C), :] = sides[C * x : C * x + C, 128:]
            return carry

        lax.fori_loop(0, BR, edges, 0)

    def convolve(z, n, g, store, done):
        live = jnp.concatenate([alive[g]] * 8, axis=0) > 0.5

        def body(i, carry):
            pair = [2 * i, 2 * i + 1]
            products = []
            for y in range(BR + 2):
                at = slice(ROWS * y, ROWS * y + ROWS)
                stack = jnp.concatenate(
                    [
                        jnp.concatenate(
                            [z[g, x, at, :], z[g, x + 1, at, :]]
                            + [z[g, x + 2, ROWS * y : ROWS * y + 2 * C, :]], axis=0,
                        )
                        for x in pair
                    ], axis=1,
                )
                if y == 0:
                    lhs = wa[n, 0:C]
                elif y == BR + 1:
                    lhs = wa[n, 2 * C :]
                else:
                    lhs = wa[n]
                products.append(dot(lhs, stack))
            for y in range(BR):
                last = jnp.concatenate(
                    [
                        jnp.concatenate(
                            [
                                z[g, x + 2, ROWS * (y + d) + 2 * C : ROWS * (y + d) + 3 * C, :]
                                for d in range(3)
                            ], axis=0,
                        )
                        for x in pair
                    ], axis=1,
                )
                total = products[y][0:C] + products[y + 1][C : 2 * C]
                top = products[y + 2]
                total = total + (top if y == BR - 1 else top[2 * C :])
                total = total + dot(wb[n], last)
                for m, x in enumerate(pair):
                    value = total[:, 128 * m : 128 * m + 128] * affine[2 * n] + affine[2 * n + 1]
                    store(g, x, y, value, live)
            for x in pair:
                done(g, x)
            return carry

        lax.fori_loop(0, BR // 2, body, 0)

    def store_hidden(g, x, y, value, live):
        value = jnp.where(live, jnp.maximum(value, 0.0), 0.0)
        z2[(g,) + center(x, y)] = value.astype(BF16)

    def store_out(g, x, y, value, live):
        value = jnp.maximum(value + block(z1, g, x, y).astype(F32), 0.0)
        act[g, x, y] = jnp.where(live, value, 0.0).astype(BF16)

    def saving(g, x):
        return pltpu.make_async_copy(act.at[g, x], act_hbm.at[g, x], save_sem.at[g, x])

    def nothing(g, x):
        pass

    def save(g, x):
        saving(g, x).start()

    copies = send(z1, 0)
    fill(z1, 0)
    convolve(z1, 0, 0, store_hidden, nothing)
    receive(z1, 0, copies)
    fill(z1, 1)
    convolve(z1, 0, 1, store_hidden, nothing)
    copies = send(z2, 1)
    fill(z2, 0)
    convolve(z2, 1, 0, store_out, save)
    receive(z2, 1, copies)
    fill(z2, 1)
    convolve(z2, 1, 1, store_out, save)
    for g in range(2):
        for x in range(BR):
            saving(g, x).wait()


def leave(order_ref, act_ref, out_ref, spread):
    for n in range(16):
        both = act_ref[:, n // 8, n % 8].reshape(128, 128).T
        spread[:, n] = both.astype(F32).reshape(HALF, 8, 128)
    for p in range(HALF):
        both = spread[p].reshape(128, 128).astype(BF16).T
        out_ref[order_ref[p]] = both[0:C]
        out_ref[order_ref[p + HALF]] = both[C:]


def on_device(
    features, counts, neighbors, weight_one, weight_two, scale_one, shift_one, scale_two, shift_two
):
    hbm = pl.BlockSpec(memory_space=pltpu.HBM)
    smem = pl.BlockSpec(memory_space=pltpu.SMEM)
    act, order = pl.pallas_call(
        kernel,
        out_shape=(
            jax.ShapeDtypeStruct((2, BR, BR, C, 128), BF16),
            jax.ShapeDtypeStruct((CAP,), jnp.int32),
        ),
        in_specs=[hbm, smem] + [hbm] * 7,
        out_specs=(hbm, smem),
        scratch_shapes=[
            pltpu.VMEM((CAP, C, VOX), BF16),
            pltpu.VMEM((6, CAP), jnp.int32),
            pltpu.VMEM((2, 27, C, C), BF16),
            pltpu.VMEM((4, C), F32),
            pltpu.VMEM((2, BR + 2, ROWS * (BR + 2), 128), BF16),
            pltpu.VMEM((2, BR + 2, ROWS * (BR + 2), 128), BF16),
            pltpu.VMEM((2, 3 * C, 8 * C), BF16),
            pltpu.VMEM((2, C, 3 * C), BF16),
            pltpu.VMEM((4, C, 128), F32),
            pltpu.VMEM((2, 8, 128), F32),
            pltpu.VMEM((16, HALF, 8, 128), F32),
            pltpu.VMEM((2, BR, BR, C, 128), BF16),
            pltpu.VMEM((4, LANES, LANES), BF16),
            pltpu.VMEM((4, 128, 128), BF16),
            pltpu.VMEM((12, 128, 128), BF16),
            pltpu.VMEM((2, LANES, LANES), BF16),
            pltpu.VMEM((128, 256), BF16),
            pltpu.VMEM((2, 16, 16, 256), BF16),
            pltpu.VMEM((2, 16, 16, 256), BF16),
            pltpu.VMEM((4, 128, 128), F32),
            pltpu.VMEM((8 * C, 128), BF16),
            pltpu.SemaphoreType.DMA((8,)),
            pltpu.SemaphoreType.DMA((2, PEERS)),
            pltpu.SemaphoreType.DMA((2, PEERS)),
            pltpu.SemaphoreType.DMA((2, BR)),
        ],
        compiler_params=pltpu.CompilerParams(
            collective_id=0, has_side_effects=True, vmem_limit_bytes=61 << 20
        ),
    )(
        features, counts, neighbors, weight_one, weight_two,
        scale_one, shift_one, scale_two, shift_two,
    )
    return pl.pallas_call(
        leave,
        grid=(4,),
        out_shape=jax.ShapeDtypeStruct((CAP, C, VOX), BF16),
        in_specs=[smem, pl.BlockSpec((2, 2, BR, C, 128), lambda j: (0, j, 0, 0, 0))],
        out_specs=pl.BlockSpec((CAP, C, 128), lambda j: (0, 0, j)),
        scratch_shapes=[pltpu.VMEM((HALF, 16, 8, 128), F32)],
        compiler_params=pltpu.CompilerParams(vmem_limit_bytes=60 << 20),
    )(order, act)


def solution(mesh):
    in_specs = (P("gz", None, None), P("gz"), P(None, "gz"), P(), P(), P(), P(), P(), P())
    out_specs = P("gz", None, None)
    return jax.shard_map(
        on_device, mesh=mesh, in_specs=in_specs, out_specs=out_specs, check_vma=False
    )
```

```python
import jax
import jax.numpy as jnp
from jax import lax
from jax.experimental import pallas as pl
from jax.experimental.pallas import tpu as pltpu
from jax.sharding import PartitionSpec as P

C = 64
BR = 8
CAP = 32
HALF = CAP // 2
VOX = BR**3
LANES = CAP * BR
PARKED_SLOT = 30
PARK = PARKED_SLOT * BR
ROWS = 3 * C
OFFSETS = (1, 2, 3, 4, 5, -1, -2, -3, -4, -5, 64)
PEERS = len(OFFSETS)
INVERSE = tuple(OFFSETS.index(-o) if abs(o) < 64 else PEERS - 1 for o in OFFSETS)
F32 = jnp.float32
BF16 = jnp.bfloat16


def dot(a, b):
    return jnp.dot(a, b, preferred_element_type=F32)


def dot_nt(a, b):
    return lax.dot_general(a, b, (((1,), (1,)), ((), ())), preferred_element_type=F32)


def iota(shape, dim):
    return lax.broadcasted_iota(jnp.int32, shape, dim)


def one_hot(condition):
    return jnp.where(condition, 1.0, 0.0).astype(BF16)


def column(row):
    wide = jnp.broadcast_to(row, (C, C))
    return jnp.sum(jnp.where(iota((C, C), 0) == iota((C, C), 1), wide, 0.0), axis=1, keepdims=True)


def center(x, y):
    return x + 1, pl.ds(ROWS * (y + 1) + C, C)


def kernel(
    feat_hbm, counts_ref, nbr_hbm, w1_hbm, w2_hbm, s1_hbm, t1_hbm, s2_hbm, t2_hbm,
    spread_ref, order_ref,
    feat, nbv, w_raw, rows, z1, z2, wa, wb, affine, alive, regroup, act, turned,
    g_near, g_far, g_send, g_shift, g_inner, send_buf, recv_buf, unpack, remote,
    load_sem, send_sem, recv_sem,
):
    devices = lax.axis_size("gz")
    me = lax.axis_index("gz")
    loads = [
        pltpu.make_async_copy(feat_hbm, feat, load_sem.at[0]),
        pltpu.make_async_copy(nbr_hbm, nbv, load_sem.at[1]),
        pltpu.make_async_copy(w1_hbm, w_raw.at[0], load_sem.at[2]),
        pltpu.make_async_copy(w2_hbm, w_raw.at[1], load_sem.at[3]),
    ]
    for i, ref in enumerate((s1_hbm, t1_hbm, s2_hbm, t2_hbm)):
        loads.append(pltpu.make_async_copy(ref, rows.at[i], load_sem.at[4 + i]))
    for load in loads:
        load.start()
    peers = [lax.rem(me + (o + devices), devices) for o in OFFSETS]
    barrier = pltpu.get_barrier_semaphore()
    for peer in peers:
        pl.semaphore_signal(
            barrier, inc=1, device_id=(peer,), device_id_type=pl.DeviceIdType.MESH
        )

    corner = jnp.zeros((ROWS, 128), BF16)
    for z in (z1, z2):
        for g in range(2):
            for x in (0, BR + 1):
                for y in (0, BR + 1):
                    z[g, x, ROWS * y : ROWS * y + ROWS, :] = corner
    recv_buf[:, PEERS:] = jnp.zeros((2, 16 - PEERS, 16, 256), BF16)

    loads[1].wait()
    table = nbv[...]
    dist = ((table >> 5) - me + 2 * devices) & (devices - 1)
    peer_at = jnp.where(dist == 64, PEERS - 1, jnp.where(dist <= 5, dist - 1, 132 - dist))
    borders = jnp.where((table >= 0) & (dist != 0), 1.0, 0.0)
    borders = jnp.max(borders, axis=0, keepdims=True)
    slot = iota((1, CAP), 1)
    usable = slot < PARKED_SLOT
    flags = jnp.concatenate(
        [jnp.where(usable, borders, 0.0), jnp.where(usable, 1.0 - borders, 0.0)]
        + [jnp.zeros((6, CAP), F32)], axis=0,
    ).astype(BF16)
    ranks = dot(flags, one_hot(iota((CAP, CAP), 0) < iota((CAP, CAP), 1)))
    plain = jnp.sum(flags[1:2].astype(F32), axis=1, keepdims=True)
    place = jnp.where(borders > 0.5, plain + ranks[0:1], ranks[1:2])
    place = jnp.where(usable, place.astype(jnp.int32), slot)
    square = iota((CAP, CAP), 0) == iota((CAP, CAP), 1)
    place_column = jnp.sum(
        jnp.where(square, jnp.broadcast_to(place, (CAP, CAP)), 0), axis=1, keepdims=True
    )
    order = [jnp.sum(jnp.where(place == s, slot, 0)) for s in range(CAP)]
    order = [jnp.clip(s, 0, CAP - 1) for s in order]
    for s in range(CAP):
        order_ref[s] = order[s]

    codes = []
    for k in range(6):
        local = jnp.where(iota((CAP, CAP), 0) == (table[k : k + 1] & (CAP - 1)), place_column, 0)
        local = jnp.sum(local, axis=0, keepdims=True)
        code = jnp.where(dist[k : k + 1] == 0, local, CAP + peer_at[k : k + 1])
        codes.append(jnp.where(table[k : k + 1] < 0, -1, code))
    codes.append((slot < counts_ref[0]).astype(jnp.int32))
    codes.append(jnp.zeros((1, CAP), jnp.int32))
    codes = jnp.concatenate(codes, axis=0).astype(F32).astype(BF16)
    wide = dot(codes, one_hot(place_column == iota((CAP, LANES), 1) >> 3)).astype(jnp.int32)
    alive_row = wide[6:7]
    wide = [jnp.where(wide[k : k + 1] < 0, -4096, wide[k : k + 1] * 8) for k in range(6)]
    peer = [(wide[k] >> 3) - CAP for k in range(6)]
    lane = iota((1, LANES), 1)
    lane_z = lane & 7
    row_near = iota((LANES, LANES), 0)
    row_far = iota((128, 128), 0)
    low_edge, high_edge = lane_z == 0, lane_z == 7
    for k in range(4):
        g_near[k] = one_hot(row_near == jnp.where(peer[k] < 0, wide[k] + lane_z, -1))
        far = peer[k][:, 128:]
        z_far = lane_z[:, 128:]
        g_far[k] = one_hot(row_far == jnp.where(far < 0, -1, 16 * z_far + far))
        g_send[k] = one_hot(row_far == jnp.where(far < 0, -1, 8 * far + z_far))
    below = jnp.where(peer[4] < 0, wide[4] + 7, PARK + peer[4])
    above = jnp.where(peer[5] < 0, wide[5], PARK + peer[5])
    before = one_hot(row_near == jnp.where(low_edge, below, lane - 1))
    after = one_hot(row_near == jnp.where(high_edge, above, lane + 1))
    for g in range(2):
        cols = slice(128 * g, 128 * g + 128)
        g_shift[g] = jnp.concatenate([before[:, cols], after[:, cols]], axis=1)
    lane, edge = lane[:, 0:128], lane_z[:, 0:128]
    g_inner[:, 0:128] = one_hot(row_far == jnp.where(edge == 0, -1, lane - 1))
    g_inner[:, 128:] = one_hot(row_far == jnp.where(edge == 7, -1, lane + 1))
    for y in range(BR):
        key = jnp.where(high_edge, peer[5], jnp.where(low_edge, peer[4], -1))[:, 128:]
        g_send[4 + y] = one_hot(row_far == jnp.where(key < 0, -1, 8 * key + y))
    for i in range(2):
        alive[i] = jnp.broadcast_to(alive_row[:, 128 * i : 128 * i + 128], (8, 128)).astype(F32)

    for load in loads[2:]:
        load.wait()
    for n in range(2):
        for dy in range(3):
            pieces = [w_raw[n, 9 * (t // 3) + 3 * dy + t % 3] for t in range(8)]
            wa[n, dy * C : dy * C + C, :] = jnp.concatenate(pieces, axis=1)
        wb[n] = jnp.concatenate([w_raw[n, 20 + 3 * dy] for dy in range(3)], axis=1)
    for i in range(4):
        affine[i] = jnp.broadcast_to(column(rows[i : i + 1, :]), (C, 128))
    loads[0].wait()

    def enter(j, carry):
        cols = pl.ds(pl.multiple_of(128 * j, 128), 128)
        for p in range(HALF):
            both = jnp.concatenate([feat[order[p], :, cols], feat[order[p + HALF], :, cols]], axis=0)
            regroup[:, p] = both.T.astype(F32).reshape(HALF, 8, 128)
        for n in range(16):
            both = regroup[n].reshape(128, 128).astype(BF16).T
            x, at = center(2 * j + n // 8, n % 8)
            z1[0, x, at, :] = both[0:C]
            z1[1, x, at, :] = both[C:]
        return carry

    lax.fori_loop(0, 4, enter, 0)

    def block(z, g, x, y):
        return z[(g,) + center(x, y)]

    def both_groups(z, x, y):
        return jnp.concatenate([block(z, 0, x, y), block(z, 1, x, y)], axis=1)

    def layer(read, x=None, y=None):
        at = [(x, i) if y is None else (i, y) for i in range(BR)]
        return jnp.concatenate([read(*i) for i in at], axis=0)

    def send(z, phase):
        def read(x, y):
            return block(z, 1, x, y)

        faces = [layer(read, x=0), layer(read, x=7), layer(read, y=0), layer(read, y=7)]
        faces += [layer(read, y=y) for y in range(BR)]
        picked = jnp.zeros((8 * C, 128), F32)
        for k in range(12):
            picked = picked + dot_nt(faces[k], g_send[k])
        picked = picked.astype(BF16)
        blocks = [
            picked[128 * i : 128 * i + 128].T.astype(F32).reshape(16, 8, 128) for i in range(4)
        ]
        for i in range(2):
            pair = jnp.concatenate([blocks[2 * i], blocks[2 * i + 1]], axis=1).astype(BF16)
            send_buf[phase, :, :, 128 * i : 128 * i + 128] = pair
        if phase == 0:
            pl.semaphore_wait(barrier, PEERS)
        copies = []
        for p in range(PEERS):
            copy = pltpu.make_async_remote_copy(
                src_ref=send_buf.at[phase, p],
                dst_ref=recv_buf.at[phase, INVERSE[p]],
                send_sem=send_sem.at[phase, p],
                recv_sem=recv_sem.at[phase, INVERSE[p]],
                device_id=(peers[p],),
                device_id_type=pl.DeviceIdType.MESH,
            )
            copy.start()
            copies.append(copy)
        return copies

    def receive(z, phase, copies):
        for copy in copies:
            copy.wait()
        for i in range(2):
            pair = recv_buf[phase, :, :, 128 * i : 128 * i + 128].astype(F32)
            for h in range(2):
                unpack[2 * i + h] = pair[:, 8 * h : 8 * h + 8].reshape(128, 128)
        parked = one_hot(iota((16, 128), 1) >= PARK - 128)
        parked = jnp.concatenate([parked] * 8, axis=0) > 0
        for i in range(4):
            got = jnp.concatenate(
                [unpack[i, pl.ds(q, 16, stride=8), :] for q in range(BR)], axis=0
            )
            got = got.astype(BF16).T
            remote[128 * i : 128 * i + 128, :] = got
            for q in range(BR):
                shifted = pltpu.roll(got, PARK - 128 - 16 * q, 1) if q < 7 else got
                both = jnp.concatenate([block(z, 1, 2 * i + n, q) for n in range(2)], axis=0)
                both = jnp.where(parked, shifted, both)
                for n in range(2):
                    z[(1,) + center(2 * i + n, q)] = both[C * n : C * n + C]

    def fill(z, g):
        def read(x, y):
            return both_groups(z, x, y)

        cols = slice(128 * g, 128 * g + 128)
        for k in range(4):
            face = layer(read, x=7 - 7 * k) if k < 2 else layer(read, y=7 - 7 * (k - 2))
            halo = dot(face, g_near[k, :, cols])
            if g == 1:
                halo = halo + dot(remote[...], g_far[k])
            halo = halo.astype(BF16)
            sides = dot(halo, g_inner[...]).astype(BF16)
            for a in range(BR):
                if k < 2:
                    x, base = (BR + 1) * k, ROWS * (a + 1)
                else:
                    x, base = a + 1, ROWS * (BR + 1) * (k - 2)
                rows = slice(C * a, C * a + C)
                z[g, x, base : base + C, :] = sides[rows, 0:128]
                z[g, x, base + C : base + 2 * C, :] = halo[rows]
                z[g, x, base + 2 * C : base + 3 * C, :] = sides[rows, 128:]

        def edges(y, carry):
            sides = dot(layer(read, y=y), g_shift[g]).astype(BF16)
            base = ROWS * (y + 1)
            for x in range(BR):
                z[g, x + 1, pl.ds(base, C), :] = sides[C * x : C * x + C, 0:128]
                z[g, x + 1, pl.ds(base + 2 * C, C), :] = sides[C * x : C * x + C, 128:]
            return carry

        for y in range(BR):
            edges(y, 0)

    def convolve(z, n, g, store, done):
        live = jnp.concatenate([alive[g]] * 8, axis=0) > 0.5

        def body(i, carry):
            pair = [2 * i, 2 * i + 1]
            products = []
            for y in range(BR + 2):
                at = slice(ROWS * y, ROWS * y + ROWS)
                stack = jnp.concatenate(
                    [
                        jnp.concatenate(
                            [z[g, x, at, :], z[g, x + 1, at, :]]
                            + [z[g, x + 2, ROWS * y : ROWS * y + 2 * C, :]], axis=0,
                        )
                        for x in pair
                    ], axis=1,
                )
                if y == 0:
                    lhs = wa[n, 0:C]
                elif y == BR + 1:
                    lhs = wa[n, 2 * C :]
                else:
                    lhs = wa[n]
                products.append(dot(lhs, stack))
            for y in range(BR):
                last = jnp.concatenate(
                    [
                        jnp.concatenate(
                            [
                                z[g, x + 2, ROWS * (y + d) + 2 * C : ROWS * (y + d) + 3 * C, :]
                                for d in range(3)
                            ], axis=0,
                        )
                        for x in pair
                    ], axis=1,
                )
                total = products[y][0:C] + products[y + 1][C : 2 * C]
                top = products[y + 2]
                total = total + (top if y == BR - 1 else top[2 * C :])
                total = total + dot(wb[n], last)
                for m, x in enumerate(pair):
                    value = total[:, 128 * m : 128 * m + 128] * affine[2 * n] + affine[2 * n + 1]
                    store(g, x, y, value, live)
            for x in pair:
                done(g, x)
            return carry

        for i in range(BR // 2):
            body(i, 0)

    def store_hidden(g, x, y, value, live):
        value = jnp.where(live, jnp.maximum(value, 0.0), 0.0)
        z2[(g,) + center(x, y)] = value.astype(BF16)

    def store_out(g, x, y, value, live):
        value = jnp.maximum(value + block(z1, g, x, y).astype(F32), 0.0)
        value = jnp.where(live, value, 0.0).astype(BF16)
        if g == 0:
            act[x, y] = value
        else:
            both = jnp.concatenate([act[x, y], value], axis=0).T
            turned[x, y] = both.astype(F32).reshape(HALF, 8, 128)

    def nothing(g, x):
        pass

    def spread(g, x):
        for y in range(0, BR, 2):
            pair = jnp.concatenate([turned[x, y], turned[x, y + 1]], axis=1).astype(BF16)
            at = 64 * x + 8 * y
            spread_ref[:, at : at + 16, :] = pair

    copies = send(z1, 0)
    fill(z1, 0)
    convolve(z1, 0, 0, store_hidden, nothing)
    receive(z1, 0, copies)
    fill(z1, 1)
    convolve(z1, 0, 1, store_hidden, nothing)
    copies = send(z2, 1)
    fill(z2, 0)
    convolve(z2, 1, 0, store_out, nothing)
    receive(z2, 1, copies)
    fill(z2, 1)
    convolve(z2, 1, 1, store_out, spread)


def leave(order_ref, spread_ref, out_hbm, bricks, save_sem):
    saves = []
    for p in range(HALF):
        for j in range(4):
            both = spread_ref[p, 128 * j : 128 * j + 128, :].T
            bricks[p, :, 128 * j : 128 * j + 128] = both[0:C]
            bricks[p + HALF, :, 128 * j : 128 * j + 128] = both[C:]
        for s in (p, p + HALF):
            save = pltpu.make_async_copy(bricks.at[s], out_hbm.at[order_ref[s]], save_sem.at[s])
            save.start()
            saves.append(save)
    for save in saves:
        save.wait()


def on_device(
    features, counts, neighbors, weight_one, weight_two, scale_one, shift_one, scale_two, shift_two
):
    hbm = pl.BlockSpec(memory_space=pltpu.HBM)
    smem = pl.BlockSpec(memory_space=pltpu.SMEM)
    vmem = pl.BlockSpec(memory_space=pltpu.VMEM)
    arrays = [features, neighbors, weight_one, weight_two]
    arrays += [scale_one, shift_one, scale_two, shift_two]
    features, *rest = [pltpu.with_memory_space_constraint(a, pltpu.HBM) for a in arrays]
    spread, order = pl.pallas_call(
        kernel,
        out_shape=(
            pltpu.VMEM((HALF, VOX, 128), BF16),
            jax.ShapeDtypeStruct((CAP,), jnp.int32),
        ),
        in_specs=[hbm, smem] + [hbm] * 7,
        out_specs=(vmem, smem),
        scratch_shapes=[
            pltpu.VMEM((CAP, C, VOX), BF16),
            pltpu.VMEM((6, CAP), jnp.int32),
            pltpu.VMEM((2, 27, C, C), BF16),
            pltpu.VMEM((4, C), F32),
            pltpu.VMEM((2, BR + 2, ROWS * (BR + 2), 128), BF16),
            pltpu.VMEM((2, BR + 2, ROWS * (BR + 2), 128), BF16),
            pltpu.VMEM((2, 3 * C, 8 * C), BF16),
            pltpu.VMEM((2, C, 3 * C), BF16),
            pltpu.VMEM((4, C, 128), F32),
            pltpu.VMEM((2, 8, 128), F32),
            pltpu.VMEM((16, HALF, 8, 128), F32),
            pltpu.VMEM((BR, BR, C, 128), BF16),
            pltpu.VMEM((BR, BR, HALF, 8, 128), F32),
            pltpu.VMEM((4, LANES, LANES), BF16),
            pltpu.VMEM((4, 128, 128), BF16),
            pltpu.VMEM((12, 128, 128), BF16),
            pltpu.VMEM((2, LANES, LANES), BF16),
            pltpu.VMEM((128, 256), BF16),
            pltpu.VMEM((2, 16, 16, 256), BF16),
            pltpu.VMEM((2, 16, 16, 256), BF16),
            pltpu.VMEM((4, 128, 128), F32),
            pltpu.VMEM((8 * C, 128), BF16),
            pltpu.SemaphoreType.DMA((8,)),
            pltpu.SemaphoreType.DMA((2, PEERS)),
            pltpu.SemaphoreType.DMA((2, PEERS)),
        ],
        compiler_params=pltpu.CompilerParams(
            collective_id=0, has_side_effects=True, vmem_limit_bytes=48 << 20
        ),
    )(
        features, counts, *rest
    )
    return pl.pallas_call(
        leave,
        out_shape=jax.ShapeDtypeStruct((CAP, C, VOX), BF16),
        in_specs=[smem, vmem],
        out_specs=hbm,
        scratch_shapes=[pltpu.VMEM((CAP, C, VOX), BF16), pltpu.SemaphoreType.DMA((CAP,))],
        compiler_params=pltpu.CompilerParams(vmem_limit_bytes=8 << 20),
    )(order, spread)


def solution(mesh):
    in_specs = (P("gz", None, None), P("gz"), P(None, "gz"), P(), P(), P(), P(), P(), P())
    out_specs = P("gz", None, None)
    return jax.shard_map(
        on_device, mesh=mesh, in_specs=in_specs, out_specs=out_specs, check_vma=False
    )
```

```python
import jax
import jax.numpy as jnp
from jax import lax
from jax.experimental import pallas as pl
from jax.experimental.pallas import tpu as pltpu
from jax.sharding import PartitionSpec as P

C = 64
BR = 8
CAP = 32
HALF = CAP // 2
VOX = BR**3
LANES = CAP * BR
PARKED_SLOT = 30
PARK = PARKED_SLOT * BR
ROWS = 3 * C
OFFSETS = (1, 2, 3, 4, 5, -1, -2, -3, -4, -5, 64)
PEERS = len(OFFSETS)
INVERSE = tuple(OFFSETS.index(-o) if abs(o) < 64 else PEERS - 1 for o in OFFSETS)
F32 = jnp.float32
BF16 = jnp.bfloat16


def dot(a, b):
    return jnp.dot(a, b, preferred_element_type=F32)


def dot_nt(a, b):
    return lax.dot_general(a, b, (((1,), (1,)), ((), ())), preferred_element_type=F32)


def iota(shape, dim):
    return lax.broadcasted_iota(jnp.int32, shape, dim)


def one_hot(condition):
    return jnp.where(condition, 1.0, 0.0).astype(BF16)


def column(row):
    wide = jnp.broadcast_to(row, (C, C))
    return jnp.sum(jnp.where(iota((C, C), 0) == iota((C, C), 1), wide, 0.0), axis=1, keepdims=True)


def center(x, y):
    return x + 1, pl.ds(ROWS * (y + 1) + C, C)


def kernel(
    feat_hbm, counts_ref, nbr_hbm, w1_hbm, w2_hbm, s1_hbm, t1_hbm, s2_hbm, t2_hbm,
    spread_ref, order_ref,
    feat, nbv, w_raw, rows, z1, z2, wa, wb, affine, alive, regroup, act, turned,
    g_near, g_far, g_send, g_shift, send_buf, recv_buf, unpack, remote,
    load_sem, send_sem, recv_sem,
):
    devices = lax.axis_size("gz")
    me = lax.axis_index("gz")
    loads = [
        pltpu.make_async_copy(feat_hbm, feat, load_sem.at[0]),
        pltpu.make_async_copy(nbr_hbm, nbv, load_sem.at[1]),
        pltpu.make_async_copy(w1_hbm, w_raw.at[0], load_sem.at[2]),
        pltpu.make_async_copy(w2_hbm, w_raw.at[1], load_sem.at[3]),
    ]
    for i, ref in enumerate((s1_hbm, t1_hbm, s2_hbm, t2_hbm)):
        loads.append(pltpu.make_async_copy(ref, rows.at[i], load_sem.at[4 + i]))
    for load in loads:
        load.start()
    peers = [lax.rem(me + (o + devices), devices) for o in OFFSETS]
    barrier = pltpu.get_barrier_semaphore()
    for peer in peers:
        pl.semaphore_signal(
            barrier, inc=1, device_id=(peer,), device_id_type=pl.DeviceIdType.MESH
        )

    recv_buf[:, PEERS:] = jnp.zeros((2, 16 - PEERS, 16, 256), BF16)

    for load in loads:
        load.wait()
    for n in range(2):
        for dy in range(3):
            pieces = [w_raw[n, 9 * (t // 3) + 3 * dy + t % 3] for t in range(8)]
            wa[n, dy * C : dy * C + C, :] = jnp.concatenate(pieces, axis=1)
        wb[n] = jnp.concatenate([w_raw[n, 20 + 3 * dy] for dy in range(3)], axis=1)
    for i in range(4):
        affine[i] = jnp.broadcast_to(column(rows[i : i + 1, :]), (C, 128))
    table = nbv[...]
    dist = ((table >> 5) - me + 2 * devices) & (devices - 1)
    peer_at = jnp.where(dist == 64, PEERS - 1, jnp.where(dist <= 5, dist - 1, 132 - dist))
    borders = jnp.where((table >= 0) & (dist != 0), 1.0, 0.0)
    borders = jnp.max(borders, axis=0, keepdims=True)
    slot = iota((1, CAP), 1)
    usable = slot < PARKED_SLOT
    flags = jnp.concatenate(
        [jnp.where(usable, borders, 0.0), jnp.where(usable, 1.0 - borders, 0.0)]
        + [jnp.zeros((6, CAP), F32)], axis=0,
    ).astype(BF16)
    ranks = dot(flags, one_hot(iota((CAP, CAP), 0) < iota((CAP, CAP), 1)))
    plain = jnp.sum(flags[1:2].astype(F32), axis=1, keepdims=True)
    place = jnp.where(borders > 0.5, plain + ranks[0:1], ranks[1:2])
    place = jnp.where(usable, place.astype(jnp.int32), slot)
    square = iota((CAP, CAP), 0) == iota((CAP, CAP), 1)
    place_column = jnp.sum(
        jnp.where(square, jnp.broadcast_to(place, (CAP, CAP)), 0), axis=1, keepdims=True
    )
    order = [jnp.sum(jnp.where(place == s, slot, 0)) for s in range(CAP)]
    order = [jnp.clip(s, 0, CAP - 1) for s in order]
    for s in range(CAP):
        order_ref[s] = order[s]

    codes = []
    for k in range(6):
        local = jnp.where(iota((CAP, CAP), 0) == (table[k : k + 1] & (CAP - 1)), place_column, 0)
        local = jnp.sum(local, axis=0, keepdims=True)
        code = jnp.where(dist[k : k + 1] == 0, local, CAP + peer_at[k : k + 1])
        codes.append(jnp.where(table[k : k + 1] < 0, -1, code))
    codes.append((slot < counts_ref[0]).astype(jnp.int32))
    codes.append(jnp.zeros((1, CAP), jnp.int32))
    codes = jnp.concatenate(codes, axis=0).astype(F32).astype(BF16)
    wide = dot(codes, one_hot(place_column == iota((CAP, LANES), 1) >> 3)).astype(jnp.int32)
    alive_row = wide[6:7]
    wide = [jnp.where(wide[k : k + 1] < 0, -4096, wide[k : k + 1] * 8) for k in range(6)]
    peer = [(wide[k] >> 3) - CAP for k in range(6)]
    lane = iota((1, LANES), 1)
    lane_z = lane & 7
    row_far = iota((128, 128), 0)
    low_edge, high_edge = lane_z == 0, lane_z == 7
    for k in range(4):
        far = peer[k][:, 128:]
        half = slice(128 * (k % 2), 128 * (k % 2) + 128)
        key = jnp.where(far < 0, -1, 8 * far + lane_z[:, 128:])
        g_send[k // 2, :, half] = one_hot(row_far == key)
    for y in range(BR):
        key = jnp.where(high_edge, peer[5], jnp.where(low_edge, peer[4], -1))[:, 128:]
        half = slice(128 * (y % 2), 128 * (y % 2) + 128)
        g_send[2 + y // 2, :, half] = one_hot(row_far == jnp.where(key < 0, -1, 8 * key + y))

    def enter(j, carry):
        cols = slice(128 * j, 128 * j + 128)
        for p in range(HALF):
            both = jnp.concatenate([feat[order[p], :, cols], feat[order[p + HALF], :, cols]], axis=0)
            regroup[:, p] = both.T.astype(F32).reshape(HALF, 8, 128)
        for n in range(16):
            both = regroup[n].reshape(128, 128).astype(BF16).T
            x, at = center(2 * j + n // 8, n % 8)
            z1[0, x, at, :] = both[0:C]
            z1[1, x, at, :] = both[C:]
        return carry

    for j in range(4):
        enter(j, 0)

    def block(z, g, x, y):
        return z[(g,) + center(x, y)]

    def both_groups(z, x, y):
        return jnp.concatenate([block(z, 0, x, y), block(z, 1, x, y)], axis=1)

    def layer(read, x=None, y=None):
        at = [(x, i) if y is None else (i, y) for i in range(BR)]
        return jnp.concatenate([read(*i) for i in at], axis=0)

    def send(z, phase):
        def read(x, y):
            return block(z, 1, x, y)

        faces = [layer(read, x=0), layer(read, x=7), layer(read, y=0), layer(read, y=7)]
        faces += [layer(read, y=y) for y in range(BR)]
        picked = jnp.zeros((8 * C, 128), F32)
        for k in range(6):
            pair = jnp.concatenate(faces[2 * k : 2 * k + 2], axis=1)
            picked = picked + dot_nt(pair, g_send[k])
        picked = picked.astype(BF16)
        blocks = [
            picked[128 * i : 128 * i + 128].T.astype(F32).reshape(16, 8, 128) for i in range(4)
        ]
        for i in range(2):
            pair = jnp.concatenate([blocks[2 * i], blocks[2 * i + 1]], axis=1).astype(BF16)
            send_buf[phase, :, :, 128 * i : 128 * i + 128] = pair
        if phase == 0:
            pl.semaphore_wait(barrier, PEERS)
        copies = []
        for p in range(PEERS):
            copy = pltpu.make_async_remote_copy(
                src_ref=send_buf.at[phase, p],
                dst_ref=recv_buf.at[phase, INVERSE[p]],
                send_sem=send_sem.at[phase, p],
                recv_sem=recv_sem.at[phase, INVERSE[p]],
                device_id=(peers[p],),
                device_id_type=pl.DeviceIdType.MESH,
            )
            copy.start()
            copies.append(copy)
        return copies

    def receive(z, phase, copies):
        for copy in copies:
            copy.wait()
        for i in range(2):
            pair = recv_buf[phase, :, :, 128 * i : 128 * i + 128].astype(F32)
            for h in range(2):
                unpack[2 * i + h] = pair[:, 8 * h : 8 * h + 8].reshape(128, 128)
        parked = one_hot(iota((16, 128), 1) >= PARK - 128)
        parked = jnp.concatenate([parked] * 8, axis=0) > 0
        for i in range(4):
            got = jnp.concatenate(
                [unpack[i, pl.ds(q, 16, stride=8), :] for q in range(BR)], axis=0
            )
            got = got.astype(BF16).T
            remote[128 * i : 128 * i + 128, :] = got
            for q in range(BR):
                shifted = pltpu.roll(got, PARK - 128 - 16 * q, 1) if q < 7 else got
                both = jnp.concatenate([block(z, 1, 2 * i + n, q) for n in range(2)], axis=0)
                both = jnp.where(parked, shifted, both)
                for n in range(2):
                    z[(1,) + center(2 * i + n, q)] = both[C * n : C * n + C]

    low_lanes = one_hot((iota((16, 128), 1) & 7) == 0)
    high_lanes = one_hot((iota((16, 128), 1) & 7) == 7)

    def fill(z, g):
        def read(x, y):
            return both_groups(z, x, y)

        def planes(k, a):
            if k < 2:
                return (BR + 1) * k, ROWS * (a + 1)
            return a + 1, ROWS * (BR + 1) * (k - 2)

        def put(x, base, value):
            low = jnp.concatenate([low_lanes] * (C // 16), axis=0) > 0
            high = jnp.concatenate([high_lanes] * (C // 16), axis=0) > 0
            zero = jnp.zeros((C, 128), BF16)
            z[g, x, base : base + C, :] = jnp.where(low, zero, pltpu.roll(value, 1, 1))
            z[g, x, base + C : base + 2 * C, :] = value
            z[g, x, base + 2 * C : base + 3 * C, :] = jnp.where(high, zero, pltpu.roll(value, 127, 1))

        if g == 0:
            for k in range(4):
                face = layer(read, x=7 - 7 * k) if k < 2 else layer(read, y=7 - 7 * (k - 2))
                halo = dot(face, g_near[k]).astype(BF16)
                for a in range(BR):
                    x, base = planes(k, a)
                    put(x, base, halo[C * a : C * a + C, 0:128])
                    z[1, x, base + C : base + 2 * C, :] = halo[C * a : C * a + C, 128:]
        else:
            far = dot(remote[...], g_far[...]).astype(BF16)
            for k in range(4):
                for a in range(BR):
                    x, base = planes(k, a)
                    local = z[1, x, base + C : base + 2 * C, :]
                    put(x, base, local + far[C * a : C * a + C, 128 * k : 128 * k + 128])

        def edges(y, carry):
            sides = dot(layer(read, y=y), g_shift[g]).astype(BF16)
            base = ROWS * (y + 1)
            for x in range(BR):
                z[g, x + 1, pl.ds(base, C), :] = sides[C * x : C * x + C, 0:128]
                z[g, x + 1, pl.ds(base + 2 * C, C), :] = sides[C * x : C * x + C, 128:]
            return carry

        for y in range(BR):
            edges(y, 0)

    def convolve(z, n, g, store, done):
        live = jnp.concatenate([alive[g]] * 8, axis=0) > 0.5

        def body(i, carry):
            pair = [2 * i, 2 * i + 1]
            products = []
            for y in range(BR + 2):
                at = slice(ROWS * y, ROWS * y + ROWS)
                stack = jnp.concatenate(
                    [
                        jnp.concatenate(
                            [z[g, x, at, :], z[g, x + 1, at, :]]
                            + [z[g, x + 2, ROWS * y : ROWS * y + 2 * C, :]], axis=0,
                        )
                        for x in pair
                    ], axis=1,
                )
                if y == 0:
                    lhs = wa[n, 0:C]
                elif y == BR + 1:
                    lhs = wa[n, 2 * C :]
                else:
                    lhs = wa[n]
                products.append(dot(lhs, stack))
            for y in range(BR):
                last = jnp.concatenate(
                    [
                        jnp.concatenate(
                            [
                                z[g, x + 2, ROWS * (y + d) + 2 * C : ROWS * (y + d) + 3 * C, :]
                                for d in range(3)
                            ], axis=0,
                        )
                        for x in pair
                    ], axis=1,
                )
                total = products[y][0:C] + products[y + 1][C : 2 * C]
                top = products[y + 2]
                total = total + (top if y == BR - 1 else top[2 * C :])
                total = total + dot(wb[n], last)
                for m, x in enumerate(pair):
                    value = total[:, 128 * m : 128 * m + 128] * affine[2 * n] + affine[2 * n + 1]
                    store(g, x, y, value, live)
            for x in pair:
                done(g, x)
            return carry

        for i in range(BR // 2):
            body(i, 0)

    def store_hidden(g, x, y, value, live):
        value = jnp.where(live, jnp.maximum(value, 0.0), 0.0)
        z2[(g,) + center(x, y)] = value.astype(BF16)

    def store_out(g, x, y, value, live):
        value = jnp.maximum(value + block(z1, g, x, y).astype(F32), 0.0)
        value = jnp.where(live, value, 0.0).astype(BF16)
        if g == 0:
            act[x, y] = value
        else:
            both = jnp.concatenate([act[x, y], value], axis=0).T
            turned[x, y] = both.astype(F32).reshape(HALF, 8, 128)

    def nothing(g, x):
        pass

    def spread(g, x):
        for y in range(0, BR, 2):
            pair = jnp.concatenate([turned[x, y], turned[x, y + 1]], axis=1).astype(BF16)
            at = 64 * x + 8 * y
            spread_ref[:, at : at + 16, :] = pair

    row_near = iota((LANES, LANES), 0)
    for k in range(4):
        g_near[k] = one_hot(row_near == jnp.where(peer[k] < 0, wide[k] + lane_z, -1))
        far = peer[k][:, 128:]
        key = jnp.where(far < 0, -1, 16 * lane_z[:, 128:] + far)
        g_far[:, 128 * k : 128 * k + 128] = one_hot(row_far == key)
    below = jnp.where(peer[4] < 0, wide[4] + 7, PARK + peer[4])
    above = jnp.where(peer[5] < 0, wide[5], PARK + peer[5])
    before = one_hot(row_near == jnp.where(low_edge, below, lane - 1))
    after = one_hot(row_near == jnp.where(high_edge, above, lane + 1))
    for g in range(2):
        cols = slice(128 * g, 128 * g + 128)
        g_shift[g] = jnp.concatenate([before[:, cols], after[:, cols]], axis=1)
    for i in range(2):
        alive[i] = jnp.broadcast_to(alive_row[:, 128 * i : 128 * i + 128], (8, 128)).astype(F32)

    corner = jnp.zeros((ROWS, 128), BF16)
    for z in (z1, z2):
        for g in range(2):
            for x in (0, BR + 1):
                for y in (0, BR + 1):
                    z[g, x, ROWS * y : ROWS * y + ROWS, :] = corner
    copies = send(z1, 0)
    fill(z1, 0)
    convolve(z1, 0, 0, store_hidden, nothing)
    receive(z1, 0, copies)
    fill(z1, 1)
    convolve(z1, 0, 1, store_hidden, nothing)
    copies = send(z2, 1)
    fill(z2, 0)
    convolve(z2, 1, 0, store_out, nothing)
    receive(z2, 1, copies)
    fill(z2, 1)
    convolve(z2, 1, 1, store_out, spread)


def leave(order_ref, spread_ref, out_hbm, bricks, save_sem):
    saves = []
    for p in range(HALF):
        for j in range(4):
            both = spread_ref[p, 128 * j : 128 * j + 128, :].T
            bricks[p, :, 128 * j : 128 * j + 128] = both[0:C]
            bricks[p + HALF, :, 128 * j : 128 * j + 128] = both[C:]
        for s in (p, p + HALF):
            save = pltpu.make_async_copy(bricks.at[s], out_hbm.at[order_ref[s]], save_sem.at[s])
            save.start()
            saves.append(save)
    for save in saves:
        save.wait()


def on_device(
    features, counts, neighbors, weight_one, weight_two, scale_one, shift_one, scale_two, shift_two
):
    hbm = pl.BlockSpec(memory_space=pltpu.HBM)
    smem = pl.BlockSpec(memory_space=pltpu.SMEM)
    vmem = pl.BlockSpec(memory_space=pltpu.VMEM)
    arrays = [features, neighbors, weight_one, weight_two]
    arrays += [scale_one, shift_one, scale_two, shift_two]
    features, *rest = [pltpu.with_memory_space_constraint(a, pltpu.HBM) for a in arrays]
    spread, order = pl.pallas_call(
        kernel,
        out_shape=(
            pltpu.VMEM((HALF, VOX, 128), BF16),
            jax.ShapeDtypeStruct((CAP,), jnp.int32),
        ),
        in_specs=[hbm, smem] + [hbm] * 7,
        out_specs=(vmem, smem),
        scratch_shapes=[
            pltpu.VMEM((CAP, C, VOX), BF16),
            pltpu.VMEM((6, CAP), jnp.int32),
            pltpu.VMEM((2, 27, C, C), BF16),
            pltpu.VMEM((4, C), F32),
            pltpu.VMEM((2, BR + 2, ROWS * (BR + 2), 128), BF16),
            pltpu.VMEM((2, BR + 2, ROWS * (BR + 2), 128), BF16),
            pltpu.VMEM((2, 3 * C, 8 * C), BF16),
            pltpu.VMEM((2, C, 3 * C), BF16),
            pltpu.VMEM((4, C, 128), F32),
            pltpu.VMEM((2, 8, 128), F32),
            pltpu.VMEM((16, HALF, 8, 128), F32),
            pltpu.VMEM((BR, BR, C, 128), BF16),
            pltpu.VMEM((BR, BR, HALF, 8, 128), F32),
            pltpu.VMEM((4, LANES, LANES), BF16),
            pltpu.VMEM((128, 512), BF16),
            pltpu.VMEM((6, 128, 256), BF16),
            pltpu.VMEM((2, LANES, LANES), BF16),
            pltpu.VMEM((2, 16, 16, 256), BF16),
            pltpu.VMEM((2, 16, 16, 256), BF16),
            pltpu.VMEM((4, 128, 128), F32),
            pltpu.VMEM((8 * C, 128), BF16),
            pltpu.SemaphoreType.DMA((8,)),
            pltpu.SemaphoreType.DMA((2, PEERS)),
            pltpu.SemaphoreType.DMA((2, PEERS)),
        ],
        compiler_params=pltpu.CompilerParams(
            collective_id=0, has_side_effects=True, vmem_limit_bytes=48 << 20
        ),
    )(
        features, counts, *rest
    )
    return pl.pallas_call(
        leave,
        out_shape=jax.ShapeDtypeStruct((CAP, C, VOX), BF16),
        in_specs=[smem, vmem],
        out_specs=hbm,
        scratch_shapes=[pltpu.VMEM((CAP, C, VOX), BF16), pltpu.SemaphoreType.DMA((CAP,))],
        compiler_params=pltpu.CompilerParams(vmem_limit_bytes=8 << 20),
    )(order, spread)


def solution(mesh):
    in_specs = (P("gz", None, None), P("gz"), P(None, "gz"), P(), P(), P(), P(), P(), P())
    out_specs = P("gz", None, None)
    return jax.shard_map(
        on_device, mesh=mesh, in_specs=in_specs, out_specs=out_specs, check_vma=False
    )
```

```python
import jax
import jax.numpy as jnp
from jax import lax
from jax.experimental import pallas as pl
from jax.experimental.pallas import tpu as pltpu
from jax.sharding import PartitionSpec as P

C = 64
BR = 8
CAP = 32
HALF = CAP // 2
VOX = BR**3
LANES = CAP * BR
PARKED_SLOT = 30
PARK = PARKED_SLOT * BR
ROWS = 3 * C
OFFSETS = (1, 2, 3, 4, 5, -1, -2, -3, -4, -5, 64)
PEERS = len(OFFSETS)
INVERSE = tuple(OFFSETS.index(-o) if abs(o) < 64 else PEERS - 1 for o in OFFSETS)
FAR_FIRST = sorted(range(PEERS), key=lambda p: -abs(OFFSETS[p]))
F32 = jnp.float32
BF16 = jnp.bfloat16


def dot(a, b):
    return jnp.dot(a, b, preferred_element_type=F32)


def dot_nt(a, b):
    return lax.dot_general(a, b, (((1,), (1,)), ((), ())), preferred_element_type=F32)


def iota(shape, dim):
    return lax.broadcasted_iota(jnp.int32, shape, dim)


def one_hot(condition):
    return jnp.where(condition, 1.0, 0.0).astype(BF16)


def column(row):
    wide = jnp.broadcast_to(row, (C, C))
    return jnp.sum(jnp.where(iota((C, C), 0) == iota((C, C), 1), wide, 0.0), axis=1, keepdims=True)


def center(x, y):
    return x + 1, pl.ds(ROWS * (y + 1) + C, C)


def kernel(
    feat_hbm, counts_ref, nbr_hbm, w1_hbm, w2_hbm, s1_hbm, t1_hbm, s2_hbm, t2_hbm,
    spread_ref, order_ref,
    feat, nbv, w_raw, rows, z1, z2, wa, wb, affine, alive, regroup, act, turned,
    g_near, g_far, g_send, g_shift, send_buf, recv_buf, unpack, remote,
    load_sem, send_sem, recv_sem,
):
    devices = lax.axis_size("gz")
    me = lax.axis_index("gz")
    loads = [
        pltpu.make_async_copy(feat_hbm, feat, load_sem.at[0]),
        pltpu.make_async_copy(nbr_hbm, nbv, load_sem.at[1]),
        pltpu.make_async_copy(w1_hbm, w_raw.at[0], load_sem.at[2]),
        pltpu.make_async_copy(w2_hbm, w_raw.at[1], load_sem.at[3]),
    ]
    for i, ref in enumerate((s1_hbm, t1_hbm, s2_hbm, t2_hbm)):
        loads.append(pltpu.make_async_copy(ref, rows.at[i], load_sem.at[4 + i]))
    for load in loads:
        load.start()
    peers = [lax.rem(me + (o + devices), devices) for o in OFFSETS]
    barrier = pltpu.get_barrier_semaphore()
    for peer in peers:
        pl.semaphore_signal(
            barrier, inc=1, device_id=(peer,), device_id_type=pl.DeviceIdType.MESH
        )

    recv_buf[:, PEERS:] = jnp.zeros((2, 16 - PEERS, 16, 256), BF16)

    for load in loads:
        load.wait()
    for n in range(2):
        for dy in range(3):
            pieces = [w_raw[n, 9 * (t // 3) + 3 * dy + t % 3] for t in range(8)]
            wa[n, dy * C : dy * C + C, :] = jnp.concatenate(pieces, axis=1)
        wb[n] = jnp.concatenate([w_raw[n, 20 + 3 * dy] for dy in range(3)], axis=1)
    for i in range(4):
        affine[i] = jnp.broadcast_to(column(rows[i : i + 1, :]), (C, 128))
    table = nbv[...]
    dist = ((table >> 5) - me + 2 * devices) & (devices - 1)
    peer_at = jnp.where(dist == 64, PEERS - 1, jnp.where(dist <= 5, dist - 1, 132 - dist))
    borders = jnp.where((table >= 0) & (dist != 0), 1.0, 0.0)
    borders = jnp.max(borders, axis=0, keepdims=True)
    slot = iota((1, CAP), 1)
    usable = slot < PARKED_SLOT
    flags = jnp.concatenate(
        [jnp.where(usable, borders, 0.0), jnp.where(usable, 1.0 - borders, 0.0)]
        + [jnp.zeros((6, CAP), F32)], axis=0,
    ).astype(BF16)
    ranks = dot(flags, one_hot(iota((CAP, CAP), 0) < iota((CAP, CAP), 1)))
    plain = jnp.sum(flags[1:2].astype(F32), axis=1, keepdims=True)
    place = jnp.where(borders > 0.5, plain + ranks[0:1], ranks[1:2])
    place = jnp.where(usable, place.astype(jnp.int32), slot)
    square = iota((CAP, CAP), 0) == iota((CAP, CAP), 1)
    place_column = jnp.sum(
        jnp.where(square, jnp.broadcast_to(place, (CAP, CAP)), 0), axis=1, keepdims=True
    )
    order = [jnp.sum(jnp.where(place == s, slot, 0)) for s in range(CAP)]
    order = [jnp.clip(s, 0, CAP - 1) for s in order]
    for s in range(CAP):
        order_ref[s] = order[s]

    codes = []
    for k in range(6):
        local = jnp.where(iota((CAP, CAP), 0) == (table[k : k + 1] & (CAP - 1)), place_column, 0)
        local = jnp.sum(local, axis=0, keepdims=True)
        code = jnp.where(dist[k : k + 1] == 0, local, CAP + peer_at[k : k + 1])
        codes.append(jnp.where(table[k : k + 1] < 0, -1, code))
    codes.append((slot < counts_ref[0]).astype(jnp.int32))
    codes.append(jnp.zeros((1, CAP), jnp.int32))
    codes = jnp.concatenate(codes, axis=0).astype(F32).astype(BF16)
    wide = dot(codes, one_hot(place_column == iota((CAP, LANES), 1) >> 3)).astype(jnp.int32)
    alive_row = wide[6:7]
    wide = [jnp.where(wide[k : k + 1] < 0, -4096, wide[k : k + 1] * 8) for k in range(6)]
    peer = [(wide[k] >> 3) - CAP for k in range(6)]
    lane = iota((1, LANES), 1)
    lane_z = lane & 7
    row_far = iota((128, 128), 0)
    low_edge, high_edge = lane_z == 0, lane_z == 7
    for k in range(4):
        far = peer[k][:, 128:]
        half = slice(128 * (k % 2), 128 * (k % 2) + 128)
        key = jnp.where(far < 0, -1, 8 * far + lane_z[:, 128:])
        g_send[k // 2, :, half] = one_hot(row_far == key)
    for y in range(BR):
        key = jnp.where(high_edge, peer[5], jnp.where(low_edge, peer[4], -1))[:, 128:]
        half = slice(128 * (y % 2), 128 * (y % 2) + 128)
        g_send[2 + y // 2, :, half] = one_hot(row_far == jnp.where(key < 0, -1, 8 * key + y))

    def enter(j, carry):
        cols = slice(128 * j, 128 * j + 128)
        for p in range(HALF):
            both = jnp.concatenate([feat[order[p], :, cols], feat[order[p + HALF], :, cols]], axis=0)
            regroup[:, p] = both.T.astype(F32).reshape(HALF, 8, 128)
        for n in range(16):
            both = regroup[n].reshape(128, 128).astype(BF16).T
            x, at = center(2 * j + n // 8, n % 8)
            z1[0, x, at, :] = both[0:C]
            z1[1, x, at, :] = both[C:]
        return carry

    for j in range(4):
        enter(j, 0)

    def block(z, g, x, y):
        return z[(g,) + center(x, y)]

    def both_groups(z, x, y):
        return jnp.concatenate([block(z, 0, x, y), block(z, 1, x, y)], axis=1)

    def layer(read, x=None, y=None):
        at = [(x, i) if y is None else (i, y) for i in range(BR)]
        return jnp.concatenate([read(*i) for i in at], axis=0)

    def send(z, phase):
        def read(x, y):
            return block(z, 1, x, y)

        faces = [layer(read, x=0), layer(read, x=7), layer(read, y=0), layer(read, y=7)]
        faces += [layer(read, y=y) for y in range(BR)]
        picked = jnp.zeros((8 * C, 128), F32)
        for k in range(6):
            pair = jnp.concatenate(faces[2 * k : 2 * k + 2], axis=1)
            picked = picked + dot_nt(pair, g_send[k])
        picked = picked.astype(BF16)
        blocks = [
            picked[128 * i : 128 * i + 128].T.astype(F32).reshape(16, 8, 128) for i in range(4)
        ]
        for i in range(2):
            pair = jnp.concatenate([blocks[2 * i], blocks[2 * i + 1]], axis=1).astype(BF16)
            send_buf[phase, :, :, 128 * i : 128 * i + 128] = pair
        if phase == 0:
            pl.semaphore_wait(barrier, PEERS)
        copies = []
        for p in FAR_FIRST:
            copy = pltpu.make_async_remote_copy(
                src_ref=send_buf.at[phase, p],
                dst_ref=recv_buf.at[phase, INVERSE[p]],
                send_sem=send_sem.at[phase, p],
                recv_sem=recv_sem.at[phase, INVERSE[p]],
                device_id=(peers[p],),
                device_id_type=pl.DeviceIdType.MESH,
            )
            copy.start()
            copies.append(copy)
        return copies

    def receive(z, phase, copies):
        for copy in copies:
            copy.wait()
        for i in range(2):
            pair = recv_buf[phase, :, :, 128 * i : 128 * i + 128].astype(F32)
            for h in range(2):
                unpack[2 * i + h] = pair[:, 8 * h : 8 * h + 8].reshape(128, 128)
        parked = one_hot(iota((16, 128), 1) >= PARK - 128)
        parked = jnp.concatenate([parked] * 8, axis=0) > 0
        for i in range(4):
            got = jnp.concatenate(
                [unpack[i, pl.ds(q, 16, stride=8), :] for q in range(BR)], axis=0
            )
            got = got.astype(BF16).T
            remote[128 * i : 128 * i + 128, :] = got
            for q in range(BR):
                shifted = pltpu.roll(got, PARK - 128 - 16 * q, 1) if q < 7 else got
                both = jnp.concatenate([block(z, 1, 2 * i + n, q) for n in range(2)], axis=0)
                both = jnp.where(parked, shifted, both)
                for n in range(2):
                    z[(1,) + center(2 * i + n, q)] = both[C * n : C * n + C]

    low_lanes = one_hot((iota((16, 128), 1) & 7) == 0)
    high_lanes = one_hot((iota((16, 128), 1) & 7) == 7)

    def fill(z, g):
        def read(x, y):
            return both_groups(z, x, y)

        def planes(k, a):
            if k < 2:
                return (BR + 1) * k, ROWS * (a + 1)
            return a + 1, ROWS * (BR + 1) * (k - 2)

        def put(x, base, value):
            low = jnp.concatenate([low_lanes] * (C // 16), axis=0) > 0
            high = jnp.concatenate([high_lanes] * (C // 16), axis=0) > 0
            zero = jnp.zeros((C, 128), BF16)
            z[g, x, base : base + C, :] = jnp.where(low, zero, pltpu.roll(value, 1, 1))
            z[g, x, base + C : base + 2 * C, :] = value
            z[g, x, base + 2 * C : base + 3 * C, :] = jnp.where(high, zero, pltpu.roll(value, 127, 1))

        if g == 0:
            for k in range(4):
                face = layer(read, x=7 - 7 * k) if k < 2 else layer(read, y=7 - 7 * (k - 2))
                halo = dot(face, g_near[k]).astype(BF16)
                for a in range(BR):
                    x, base = planes(k, a)
                    put(x, base, halo[C * a : C * a + C, 0:128])
                    z[1, x, base + C : base + 2 * C, :] = halo[C * a : C * a + C, 128:]
        else:
            far = dot(remote[...], g_far[...]).astype(BF16)
            for k in range(4):
                for a in range(BR):
                    x, base = planes(k, a)
                    local = z[1, x, base + C : base + 2 * C, :]
                    put(x, base, local + far[C * a : C * a + C, 128 * k : 128 * k + 128])

        def edges(y, carry):
            sides = dot(layer(read, y=y), g_shift[g]).astype(BF16)
            base = ROWS * (y + 1)
            for x in range(BR):
                z[g, x + 1, pl.ds(base, C), :] = sides[C * x : C * x + C, 0:128]
                z[g, x + 1, pl.ds(base + 2 * C, C), :] = sides[C * x : C * x + C, 128:]
            return carry

        for y in range(BR):
            edges(y, 0)

    def convolve(z, n, g, store, done):
        live = jnp.concatenate([alive[g]] * 8, axis=0) > 0.5

        def body(i, carry):
            pair = [2 * i, 2 * i + 1]
            products = []
            for y in range(BR + 2):
                at = slice(ROWS * y, ROWS * y + ROWS)
                stack = jnp.concatenate(
                    [
                        jnp.concatenate(
                            [z[g, x, at, :], z[g, x + 1, at, :]]
                            + [z[g, x + 2, ROWS * y : ROWS * y + 2 * C, :]], axis=0,
                        )
                        for x in pair
                    ], axis=1,
                )
                if y == 0:
                    lhs = wa[n, 0:C]
                elif y == BR + 1:
                    lhs = wa[n, 2 * C :]
                else:
                    lhs = wa[n]
                products.append(dot(lhs, stack))
            for y in range(BR):
                last = jnp.concatenate(
                    [
                        jnp.concatenate(
                            [
                                z[g, x + 2, ROWS * (y + d) + 2 * C : ROWS * (y + d) + 3 * C, :]
                                for d in range(3)
                            ], axis=0,
                        )
                        for x in pair
                    ], axis=1,
                )
                total = products[y][0:C] + products[y + 1][C : 2 * C]
                top = products[y + 2]
                total = total + (top if y == BR - 1 else top[2 * C :])
                total = total + dot(wb[n], last)
                for m, x in enumerate(pair):
                    value = total[:, 128 * m : 128 * m + 128] * affine[2 * n] + affine[2 * n + 1]
                    store(g, x, y, value, live)
            for x in pair:
                done(g, x)
            return carry

        for i in range(BR // 2):
            body(i, 0)

    def store_hidden(g, x, y, value, live):
        value = jnp.where(live, jnp.maximum(value, 0.0), 0.0)
        z2[(g,) + center(x, y)] = value.astype(BF16)

    def store_out(g, x, y, value, live):
        value = jnp.maximum(value + block(z1, g, x, y).astype(F32), 0.0)
        value = jnp.where(live, value, 0.0).astype(BF16)
        if g == 0:
            act[x, y] = value
        else:
            both = jnp.concatenate([act[x, y], value], axis=0).T
            turned[x, y] = both.astype(F32).reshape(HALF, 8, 128)

    def nothing(g, x):
        pass

    def spread(g, x):
        for y in range(0, BR, 2):
            pair = jnp.concatenate([turned[x, y], turned[x, y + 1]], axis=1).astype(BF16)
            at = 64 * x + 8 * y
            spread_ref[:, at : at + 16, :] = pair

    row_near = iota((LANES, LANES), 0)
    for k in range(4):
        g_near[k] = one_hot(row_near == jnp.where(peer[k] < 0, wide[k] + lane_z, -1))
        far = peer[k][:, 128:]
        key = jnp.where(far < 0, -1, 16 * lane_z[:, 128:] + far)
        g_far[:, 128 * k : 128 * k + 128] = one_hot(row_far == key)
    below = jnp.where(peer[4] < 0, wide[4] + 7, PARK + peer[4])
    above = jnp.where(peer[5] < 0, wide[5], PARK + peer[5])
    before = one_hot(row_near == jnp.where(low_edge, below, lane - 1))
    after = one_hot(row_near == jnp.where(high_edge, above, lane + 1))
    for g in range(2):
        cols = slice(128 * g, 128 * g + 128)
        g_shift[g] = jnp.concatenate([before[:, cols], after[:, cols]], axis=1)
    for i in range(2):
        alive[i] = jnp.broadcast_to(alive_row[:, 128 * i : 128 * i + 128], (8, 128)).astype(F32)

    corner = jnp.zeros((ROWS, 128), BF16)
    for z in (z1, z2):
        for g in range(2):
            for x in (0, BR + 1):
                for y in (0, BR + 1):
                    z[g, x, ROWS * y : ROWS * y + ROWS, :] = corner
    copies = send(z1, 0)
    fill(z1, 0)
    convolve(z1, 0, 0, store_hidden, nothing)
    receive(z1, 0, copies)
    fill(z1, 1)
    convolve(z1, 0, 1, store_hidden, nothing)
    copies = send(z2, 1)
    fill(z2, 0)
    convolve(z2, 1, 0, store_out, nothing)
    receive(z2, 1, copies)
    fill(z2, 1)
    convolve(z2, 1, 1, store_out, spread)


def leave(order_ref, spread_ref, out_hbm, bricks, save_sem):
    saves = []
    for p in range(HALF):
        for j in range(4):
            both = spread_ref[p, 128 * j : 128 * j + 128, :].T
            bricks[p, :, 128 * j : 128 * j + 128] = both[0:C]
            bricks[p + HALF, :, 128 * j : 128 * j + 128] = both[C:]
        for s in (p, p + HALF):
            save = pltpu.make_async_copy(bricks.at[s], out_hbm.at[order_ref[s]], save_sem.at[s])
            save.start()
            saves.append(save)
    for save in saves:
        save.wait()


def on_device(
    features, counts, neighbors, weight_one, weight_two, scale_one, shift_one, scale_two, shift_two
):
    hbm = pl.BlockSpec(memory_space=pltpu.HBM)
    smem = pl.BlockSpec(memory_space=pltpu.SMEM)
    vmem = pl.BlockSpec(memory_space=pltpu.VMEM)
    arrays = [features, neighbors, weight_one, weight_two]
    arrays += [scale_one, shift_one, scale_two, shift_two]
    features, *rest = [pltpu.with_memory_space_constraint(a, pltpu.HBM) for a in arrays]
    spread, order = pl.pallas_call(
        kernel,
        out_shape=(
            pltpu.VMEM((HALF, VOX, 128), BF16),
            jax.ShapeDtypeStruct((CAP,), jnp.int32),
        ),
        in_specs=[hbm, smem] + [hbm] * 7,
        out_specs=(vmem, smem),
        scratch_shapes=[
            pltpu.VMEM((CAP, C, VOX), BF16),
            pltpu.VMEM((6, CAP), jnp.int32),
            pltpu.VMEM((2, 27, C, C), BF16),
            pltpu.VMEM((4, C), F32),
            pltpu.VMEM((2, BR + 2, ROWS * (BR + 2), 128), BF16),
            pltpu.VMEM((2, BR + 2, ROWS * (BR + 2), 128), BF16),
            pltpu.VMEM((2, 3 * C, 8 * C), BF16),
            pltpu.VMEM((2, C, 3 * C), BF16),
            pltpu.VMEM((4, C, 128), F32),
            pltpu.VMEM((2, 8, 128), F32),
            pltpu.VMEM((16, HALF, 8, 128), F32),
            pltpu.VMEM((BR, BR, C, 128), BF16),
            pltpu.VMEM((BR, BR, HALF, 8, 128), F32),
            pltpu.VMEM((4, LANES, LANES), BF16),
            pltpu.VMEM((128, 512), BF16),
            pltpu.VMEM((6, 128, 256), BF16),
            pltpu.VMEM((2, LANES, LANES), BF16),
            pltpu.VMEM((2, 16, 16, 256), BF16),
            pltpu.VMEM((2, 16, 16, 256), BF16),
            pltpu.VMEM((4, 128, 128), F32),
            pltpu.VMEM((8 * C, 128), BF16),
            pltpu.SemaphoreType.DMA((8,)),
            pltpu.SemaphoreType.DMA((2, PEERS)),
            pltpu.SemaphoreType.DMA((2, PEERS)),
        ],
        compiler_params=pltpu.CompilerParams(
            collective_id=0, has_side_effects=True, vmem_limit_bytes=48 << 20
        ),
    )(
        features, counts, *rest
    )
    return pl.pallas_call(
        leave,
        out_shape=jax.ShapeDtypeStruct((CAP, C, VOX), BF16),
        in_specs=[smem, vmem],
        out_specs=hbm,
        scratch_shapes=[pltpu.VMEM((CAP, C, VOX), BF16), pltpu.SemaphoreType.DMA((CAP,))],
        compiler_params=pltpu.CompilerParams(vmem_limit_bytes=8 << 20),
    )(order, spread)


def solution(mesh):
    in_specs = (P("gz", None, None), P("gz"), P(None, "gz"), P(), P(), P(), P(), P(), P())
    out_specs = P("gz", None, None)
    return jax.shard_map(
        on_device, mesh=mesh, in_specs=in_specs, out_specs=out_specs, check_vma=False
    )
```
